1024 devices in a mesh: grp: 16 (over z, core), dev: 64 (over y, x).
Axes of the slice: x: 8, y: 8, z: 8, core: 2. Of those that a mesh axis runs over, the one named last changes fastest.
Arguments:
- atm_state: float32 [16, 64, 128, 1024], P('grp', 'dev'), may hold values from -6 to 6
- atm_nbrs: int32 [16, 64, 4, 1024], P('grp', 'dev'), may hold values from 0 to 1279
- atm_send: int32 [16, 64, 256], P('grp', 'dev'), may hold values from 0 to 1023
- atm_mix: float32 [16, 64, 1024], P('grp', 'dev'), may hold values from 0.2 to 0.6
- flux_weight: float32 [24, 128], replicated, may hold values from -0.5 to 0.5
- margin_counts: int32 [16, 64, 1024], P('grp', 'dev'), may hold values from 1 to 4, 1536 in all within a row
- margin_weight: float32 [16, 64, 1536], P('grp', 'dev'), may hold values from 0.05 to 1
- block_owner: int32 [16, 64, 12, 1], P('grp', 'dev'), may hold values from 0 to 7, as said below
- recv_cols: int32 [16, 64, 8, 4, 128], P('grp', 'dev'), may hold values from 0 to 2047
- ocn_state: float32 [16, 64, 80, 2048], P('grp', 'dev'), may hold values from -6 to 6
- ocn_nbrs: int32 [16, 64, 6, 2048], P('grp', 'dev'), may hold values from 0 to 2303
- ocn_send: int32 [16, 64, 256], P('grp', 'dev'), may hold values from 0 to 2047
- ocn_mix: float32 [16, 64, 2048], P('grp', 'dev'), may hold values from 0.1 to 0.4
- force_weight: float32 [80, 24], replicated, may hold values from -1.25 to 1.25
- ret_weight: float32 [12, 80], replicated, may hold values from -0.625 to 0.625
Outputs:
- atm_next: float32 [16, 64, 128, 1024], P('grp', 'dev')
- ocn_next: float32 [16, 64, 80, 2048], P('grp', 'dev')
- atm_remapped: float32 [16, 64, 12, 1024], P('grp', 'dev')
The draws below stay inside these ranges and needn't reach their ends.
Inputs may be any that keep to these rules, and one draw needn't show every extreme that they name: `margin_counts`: the 1024 counts of one partition sum to 1536, and one of them equals 4. `block_owner`: no partition sends more than 4 of its 12 blocks to one ocean group, and every partition sends exactly 4 blocks to one of them.
All inputs are finite; a program needn't handle non-finite values.
Results may differ from the reference program's by a relative error of at most 0.0029.
Values may be sent and summed in bfloat16 or wider, within the bound.
No kernel may reach another device: no remote copies, remote signals or barrier semaphores. Data moves between devices by JAX's collectives and lax.ppermute only.
A program may use at most 32 MiB of HBM per device.

```python
import math
import jax
import jax.numpy as jnp
import numpy as np
from jax import lax

LEV_A = 128
LEV_O = 80
FLUX = 24
RET = 12
KA = 4
KO = 6
BLOCK = 128
HS = 128
COLS = 1024
CELLS = 2048
ROWS = 1536
NB = 12
ATM_GRPS = 8
OCN_GRPS = 8
CAP = 4
N_GRP = 16
N_DEV = 64


def draw_block_owner(key, part):
    first_key, second_key = jax.random.split(jax.random.fold_in(key, 7311))
    partitions = N_GRP * N_DEV
    orders = jax.vmap(lambda k: jax.random.permutation(k, OCN_GRPS))(jax.random.split(first_key, partitions))
    listed = jnp.repeat(orders, CAP, axis=1)[:, :NB]
    shuffled = jax.vmap(lambda k, row: jax.random.permutation(k, row))(jax.random.split(second_key, partitions), listed)
    return shuffled.reshape(N_GRP, N_DEV, NB, 1).astype(jnp.int32)


def with_ends(array, key, least, top_value):
    spot = [jax.random.randint(jax.random.fold_in(key, axis), (), 0, length) for axis, length in enumerate(array.shape)]
    widest = array.shape.index(max(array.shape))
    next_to = spot[:widest] + [(spot[widest] + 1) % array.shape[widest]] + spot[widest + 1:]
    return array.at[tuple(spot)].set(least).at[tuple(next_to)].set(top_value)


def block_scale(own_key, dims, pieces, low, largest):
    factor_of = 1.0
    for position, parts in pieces:
        draws = jax.random.uniform(jax.random.fold_in(jax.random.fold_in(own_key, 6), position), (parts,), jnp.float32, low / len(pieces), largest / len(pieces))
        factor_of = factor_of * jnp.repeat(jnp.exp(draws), dims[position] // parts).reshape((-1,) + (1,) * (len(dims) - 1 - position))
    return factor_of


def length_profile(amount, total, most, slope):
    weights = [(1 << 20) // math.isqrt(standing ** slope) + 1 for standing in range(2, amount + 1)]
    spare, given = total - most - (amount - 1), [1] * (amount - 1)
    while spare > 0:
        candidates = [i for i in range(amount - 1) if given[i] < most]
        whole, left = sum([weights[i] for i in candidates]), spare
        for i in candidates:
            addition = min(most - given[i], max(1, left * weights[i] // whole), spare)
            given[i] = given[i] + addition
            spare = spare - addition
    return np.array([most] + given)


def ragged(stream_key, number_of, total, reach, skew):
    if number_of == 2:
        one = jax.random.randint(stream_key, (), max(1, total - reach), min(reach, total - 1) + 1)
        return jnp.stack([one, total - one])
    sizes = jnp.asarray(length_profile(number_of, total, reach, skew), jnp.int32)
    couples = (number_of - 1) // 2
    source_of, sink = sizes[1:1 + 2 * couples:2], sizes[2:2 + 2 * couples:2]
    slack = jnp.minimum(source_of - 1, reach - sink)
    passed = jax.random.randint(jax.random.fold_in(stream_key, 1), (couples,), 0, 1 << 20) % (slack + 1)
    sizes = sizes.at[1:1 + 2 * couples:2].set(source_of - passed).at[2:2 + 2 * couples:2].set(sink + passed)
    return sizes[jax.random.permutation(jax.random.fold_in(stream_key, 2), number_of)]


def bell_draw(rng, dims, deviation, most, pieces=(), held_as=jnp.bfloat16):
    drawn = deviation * jax.random.normal(rng, dims, jnp.float32)
    if pieces:
        drawn = drawn * block_scale(rng, dims, pieces, -0.22, 0.18)
    return jnp.clip(drawn, -most, most).astype(held_as)


def setup_inputs(seed: int = 0) -> dict:
    key_of = jax.random.split(jax.random.key(seed), 16)
    return {
        "atm_state": bell_draw(key_of[0], (N_GRP, N_DEV, LEV_A, COLS), 1.0, 6.0, ((0, 16), (1, 64)), jnp.float32),
        "atm_nbrs": with_ends(jax.random.randint(key_of[1], (N_GRP, N_DEV, KA, COLS), 0, COLS + 2 * HS), jax.random.fold_in(key_of[1], 1), 0, (COLS + 2 * HS) - 1).astype(jnp.int32),
        "atm_send": with_ends(jax.random.randint(key_of[2], (N_GRP, N_DEV, 2 * HS), 0, COLS), jax.random.fold_in(key_of[2], 1), 0, COLS - 1).astype(jnp.int32),
        "atm_mix": jnp.clip(0.2 + 0.400000021 * jax.random.uniform(key_of[3], (N_GRP, N_DEV, COLS), jnp.float32) ** block_scale(key_of[3], (N_GRP, N_DEV, COLS), ((0, 16), (1, 64)), -0.2, 0.2), 0.2, 0.6),
        "flux_weight": bell_draw(key_of[4], (FLUX, LEV_A), LEV_A ** -0.5, 0.5, (), jnp.float32),
        "margin_counts": jax.vmap(lambda own: ragged(own, COLS, ROWS, 4, 1))(jax.random.split(key_of[5], N_GRP * N_DEV)).reshape((N_GRP, N_DEV, COLS)).astype(jnp.int32),
        "margin_weight": jnp.clip(jnp.exp(math.log(1.0) - 2.9957323 * jax.random.uniform(key_of[6], (N_GRP, N_DEV, ROWS), jnp.float32) ** block_scale(key_of[6], (N_GRP, N_DEV, ROWS), ((0, 16), (1, 64)), -0.2, 0.2)), 0.05, 1.0),
        "block_owner": draw_block_owner(jax.random.fold_in(key_of[15], 71), 0),
        "recv_cols": with_ends(jax.random.randint(key_of[8], (N_GRP, N_DEV, ATM_GRPS, CAP, BLOCK), 0, CELLS), jax.random.fold_in(key_of[8], 1), 0, CELLS - 1).astype(jnp.int32),
        "ocn_state": bell_draw(key_of[9], (N_GRP, N_DEV, LEV_O, CELLS), 1.0, 6.0, ((0, 16), (1, 64)), jnp.float32),
        "ocn_nbrs": with_ends(jax.random.randint(key_of[10], (N_GRP, N_DEV, KO, CELLS), 0, CELLS + 2 * HS), jax.random.fold_in(key_of[10], 1), 0, (CELLS + 2 * HS) - 1).astype(jnp.int32),
        "ocn_send": with_ends(jax.random.randint(key_of[11], (N_GRP, N_DEV, 2 * HS), 0, CELLS), jax.random.fold_in(key_of[11], 1), 0, CELLS - 1).astype(jnp.int32),
        "ocn_mix": jnp.clip(0.1 + 0.3 * jax.random.uniform(key_of[12], (N_GRP, N_DEV, CELLS), jnp.float32) ** block_scale(key_of[12], (N_GRP, N_DEV, CELLS), ((0, 16), (1, 64)), -0.2, 0.2), 0.1, 0.4),
        "force_weight": bell_draw(key_of[13], (LEV_O, FLUX), FLUX ** -0.5, 1.25, (), jnp.float32),
        "ret_weight": bell_draw(key_of[14], (RET, LEV_O), LEV_O ** -0.5, 0.625, (), jnp.float32),
    }


EXACT_DOT = lax.Precision.HIGHEST


def stencil(state, pool, neighbours, mixing):
    total = jnp.take(pool, neighbours[0], axis=1)
    for which in range(1, neighbours.shape[0]):
        total = total + jnp.take(pool, neighbours[which], axis=1)
    return state + mixing[None, :] * (total / neighbours.shape[0] - state)


def pick_columns(values, indices):
    return jnp.take(values, indices, axis=1)


def pooled(state, send_list):
    half = send_list.shape[-1] // 2
    packed = jax.vmap(jax.vmap(pick_columns))(state, send_list)
    from_lower = jnp.roll(packed[..., half:], 1, axis=1)
    from_upper = jnp.roll(packed[..., :half], -1, axis=1)
    return jnp.concatenate([state, from_lower, from_upper], axis=3)


def column_ids(counts):
    return jnp.repeat(jnp.arange(COLS, dtype=jnp.int32), counts, total_repeat_length=ROWS)


def block_slots(owner):
    order = jnp.arange(owner.shape[0], dtype=jnp.int32)
    earlier = (owner[None, :] == owner[:, None]) & (order[None, :] < order[:, None])
    return jnp.sum(earlier.astype(jnp.int32), axis=1)


def remap_back(values, weights, column):
    weighted = jax.ops.segment_sum(values * weights[:, None], column, num_segments=COLS)
    weight_sum = jax.ops.segment_sum(weights, column, num_segments=COLS)
    return (weighted / weight_sum[:, None]).T


def reference(atm_state, atm_nbrs, atm_send, atm_mix, flux_weight, margin_counts, margin_weight, block_owner, recv_cols, ocn_state, ocn_nbrs, ocn_send, ocn_mix, force_weight, ret_weight):
    groups = atm_state.shape[0]
    devices = atm_state.shape[1]
    atm_groups = groups // 2
    sweep = jax.vmap(jax.vmap(stencil))
    air = atm_state[:atm_groups]
    air_next = sweep(air, pooled(air, atm_send[:atm_groups]), atm_nbrs[:atm_groups], atm_mix[:atm_groups])
    atm_next = jnp.concatenate([air_next, atm_state[atm_groups:]], axis=0)
    sea = ocn_state[atm_groups:]
    sea_base = sweep(sea, pooled(sea, ocn_send[atm_groups:]), ocn_nbrs[atm_groups:], ocn_mix[atm_groups:])
    fluxes = jnp.einsum("fl,gdlc->gdfc", flux_weight, air_next, precision=EXACT_DOT)
    column = jax.vmap(jax.vmap(column_ids))(margin_counts[:atm_groups])
    weights = margin_weight[:atm_groups]
    row_values = (jax.vmap(jax.vmap(pick_columns))(fluxes, column) * weights[:, :, None, :]).astype(jnp.bfloat16)
    owner = block_owner[:atm_groups, :, :, 0]
    slot = jax.vmap(jax.vmap(block_slots))(owner)
    sender = jnp.arange(atm_groups, dtype=jnp.int32)[:, None, None]
    partition = jnp.arange(devices, dtype=jnp.int32)[None, :, None]
    cell = recv_cols[atm_groups + owner, partition, sender, slot]
    target = ((owner * devices + partition)[..., None] * CELLS + cell).reshape(-1)
    flat_rows = row_values.reshape(atm_groups, devices, FLUX, NB, BLOCK).transpose(0, 1, 3, 4, 2).reshape(-1, FLUX).astype(jnp.float32)
    cell_flux = jnp.zeros((OCN_GRPS * devices * CELLS, FLUX), jnp.float32).at[target].add(flat_rows)
    cell_flux = cell_flux.reshape(OCN_GRPS, devices, CELLS, FLUX)
    forcing = jnp.einsum("lf,odcf->odlc", force_weight, cell_flux, precision=EXACT_DOT)
    ocn_next = jnp.concatenate([ocn_state[:atm_groups], sea_base + forcing], axis=0)
    returned = jnp.einsum("rl,odlc->odcr", ret_weight, sea, precision=EXACT_DOT).astype(jnp.bfloat16)
    looked = returned.reshape(-1, RET)[target].astype(jnp.float32).reshape(atm_groups, devices, ROWS, RET)
    remapped = jax.vmap(jax.vmap(remap_back))(looked, weights, column)
    remapped = jnp.concatenate([remapped, jnp.zeros((groups - atm_groups, devices, RET, COLS), jnp.float32)], axis=0)
    return atm_next, ocn_next, remapped
```

```python
import functools

import jax
import jax.numpy as jnp
from jax import lax
from jax.experimental import pallas as pl
from jax.experimental.pallas import tpu as pltpu
from jax.sharding import PartitionSpec as P

F32 = jnp.float32
BF16 = jnp.bfloat16
I32 = jnp.int32
TILE = 256
NT = (((1,), (1,)), ((), ()))


def dot(a, b):
    return jnp.dot(a, b, preferred_element_type=F32)


def dot_nt(a, b):
    return lax.dot_general(a, b, NT, preferred_element_type=F32)


def split(x):
    hi = x.astype(BF16)
    lo = (x - hi.astype(F32)).astype(BF16)
    return hi, lo


def exact(w, x):
    wh, wl = split(w)
    xh, xl = split(x)
    return dot(wh, xh) + (dot(wl, xh) + dot(wh, xl))


def row_iota(rows, cols):
    return lax.broadcasted_iota(I32, (rows, cols), 0)


def one_hot(rows_bf, index_row):
    return jnp.where(rows_bf == index_row, jnp.ones((), BF16), jnp.zeros((), BF16))


def pack_kernel(atm_groups, air_ref, air_send, sea_ref, sea_send, down, up, air, sea, sem):
    here = lax.axis_index("grp") < atm_groups
    half = down.shape[1]
    rows = row_iota(TILE, 2 * half).astype(F32).astype(BF16)

    def packed(state, send):
        index = send[...]
        total = None
        for base in range(0, state.shape[1], TILE):
            mark = one_hot(rows, (index - base).astype(F32).astype(BF16))
            part = dot(state[:, base : base + TILE].astype(BF16), mark)
            total = part if total is None else total + part
        levels = state.shape[0]
        out = total.astype(BF16)
        down[0:levels, :] = out[:, :half]
        up[0:levels, :] = out[:, half:]

    @pl.when(here)
    def _():
        copy = pltpu.make_async_copy(air_ref, air, sem)
        copy.start()
        copy.wait()
        packed(air, air_send)

    @pl.when(jnp.logical_not(here))
    def _():
        copy = pltpu.make_async_copy(sea_ref, sea, sem)
        copy.start()
        copy.wait()
        packed(sea, sea_send)


def stencil_chunk(pool, nbrs, at, rows, width):
    picks = [n[:, pl.ds(at, width)] for n in nbrs]
    total = None
    for base in range(0, pool.shape[1], TILE):
        marks = None
        for pick in picks:
            mark = one_hot(rows, (pick - base).astype(F32).astype(BF16))
            marks = mark if marks is None else marks + mark
        part = dot(pool[:, base : base + TILE], marks)
        total = part if total is None else total + part
    return total


def fill_ends(counts, ends):
    blocks, lanes = counts.shape
    given = counts[...].astype(F32).astype(BF16)
    upto = jnp.where(
        row_iota(lanes, lanes) <= lax.broadcasted_iota(I32, (lanes, lanes), 1), 1.0, 0.0
    ).astype(BF16)
    within = dot(given, upto)
    whole = dot(given, jnp.ones((lanes, lanes), BF16))
    before = jnp.zeros((1, lanes), F32)
    for j in range(blocks):
        ends[j : j + 1, :] = (within[j : j + 1] + before).astype(I32)
        before = before + whole[j : j + 1]


def fill_spread(counts, ends, spread):
    fill_ends(counts, ends)
    rows, _ = spread.shape
    blocks, lanes = counts.shape
    order = row_iota(rows, lanes)
    for j in range(blocks):
        end = ends[j : j + 1, :]
        begin = end - counts[j : j + 1, :]
        inside = (order >= begin) & (order < end)
        spread[:, j * lanes : (j + 1) * lanes] = jnp.where(inside, 1.0, 0.0).astype(BF16)


def slots_of(owner, seen, visit):
    for o in range(seen.shape[0]):
        seen[o] = 0
    for b in range(owner.shape[1]):
        o = owner[0, b]
        k = seen[o]
        seen[o] = k + 1
        visit(b, o, k)


def mid_kernel(
    atm_groups,
    air_ref, air_nbrs, air_mix, flux_weight, counts, weights, owner, recv,
    sea_ref, sea_nbrs, sea_mix, ret_weight, low, high,
    air_out, base_out, send_out,
    air, sea, air_pool, sea_pool, spread, ends, returned, seen, sem, out_sem,
):
    here = lax.axis_index("grp") < atm_groups
    rows = row_iota(TILE, TILE).astype(F32).astype(BF16)
    half = low.shape[1]

    def pooled(state, pool):
        levels, own = state.shape
        pool[:, :own] = state[...].astype(BF16)
        pool[:, own : own + half] = low[0:levels, :]
        pool[:, own + half :] = high[0:levels, :]

    @pl.when(here)
    def _():
        copy = pltpu.make_async_copy(air_ref, air, sem)
        copy.start()
        fill_spread(counts, ends, spread)
        send_out[...] = jnp.zeros(send_out.shape, BF16)
        copy.wait()
        pooled(air, air_pool)
        columns = air.shape[1]
        amount = air_nbrs.shape[0]
        nbrs = [air_nbrs.at[k : k + 1, :] for k in range(amount)]
        parts = []
        for at in range(0, columns, TILE):
            total = stencil_chunk(air_pool, nbrs, at, rows, TILE)
            own = air[:, at : at + TILE]
            new = own + air_mix[:, at : at + TILE] * (total * (1.0 / amount) - own)
            air[:, at : at + TILE] = new
            parts.append(exact(flux_weight[...], new))
        out_copy = pltpu.make_async_copy(air, air_out, out_sem)
        out_copy.start()
        hi, lo = split(jnp.concatenate(parts, axis=1))
        fields = hi.shape[0]
        block = send_out.shape[3]

        def visit(b, o, k):
            mark = spread[b * block : (b + 1) * block, :]
            value = dot_nt(hi, mark) + dot_nt(lo, mark)
            value = value * weights[:, b * block : (b + 1) * block]
            send_out[atm_groups + o, k] = value.astype(BF16)

        slots_of(owner, seen, visit)
        out_copy.wait()

    @pl.when(jnp.logical_not(here))
    def _():
        keep = pltpu.make_async_copy(air_ref, air_out, out_sem)
        keep.start()
        copy = pltpu.make_async_copy(sea_ref, sea, sem)
        copy.start()
        copy.wait()
        pooled(sea, sea_pool)
        cells = sea.shape[1]
        fields = ret_weight.shape[0]
        his = cells // TILE
        pad = returned.shape[0] // his
        for h in range(his):
            chunk = exact(ret_weight[...], sea[:, h * TILE : (h + 1) * TILE])
            chunk = jnp.concatenate([chunk, jnp.zeros((pad - fields, TILE), F32)], axis=0)
            returned[h * pad : (h + 1) * pad, :] = chunk.astype(BF16)
        senders, slots, block = recv.shape
        for s in range(senders):
            index = jnp.concatenate([recv[s, k : k + 1, :] for k in range(slots)], axis=1)
            top = index // TILE
            rest = (index - top * TILE).astype(F32).astype(BF16)
            row_b = row_iota(TILE, slots * block).astype(F32).astype(BF16)
            found = dot(returned[...], one_hot(row_b, rest))
            look = jnp.zeros((pad, slots * block), F32)
            for h in range(his):
                look = jnp.where(top == h, found[h * pad : (h + 1) * pad], look)
            look = jnp.concatenate(
                [look, jnp.zeros((send_out.shape[2] - pad, slots * block), F32)], axis=0
            ).astype(BF16)
            for k in range(slots):
                send_out[s, k] = look[:, k * block : (k + 1) * block]
        amount = sea_nbrs.shape[0]
        nbrs = [sea_nbrs.at[k] for k in range(amount)]

        def step(i, carry):
            at = pl.multiple_of(i * TILE, TILE)
            total = stencil_chunk(sea_pool, nbrs, at, rows, TILE)
            own = sea[:, pl.ds(at, TILE)]
            base_out[:, pl.ds(at, TILE)] = own + sea_mix[:, pl.ds(at, TILE)] * (
                total * (1.0 / amount) - own
            )
            return carry

        lax.fori_loop(0, his, step, 0)
        keep.wait()


def post_kernel(
    atm_groups,
    arrived, counts, weights, owner, recv, sea_ref, base, force_weight,
    sea_out, mapped_out,
    sea, spread, ends, mine, seen, sem,
):
    here = lax.axis_index("grp") < atm_groups

    @pl.when(here)
    def _():
        keep = pltpu.make_async_copy(sea_ref, sea_out, sem)
        keep.start()
        fill_spread(counts, ends, spread)
        fields = mapped_out.shape[0]
        block = arrived.shape[3]

        def visit(b, o, k):
            mine[:, b * block : (b + 1) * block] = arrived[atm_groups + o, k].astype(F32)

        slots_of(owner, seen, visit)
        w = weights[...]
        scaled = mine[0:16, :] * w
        order = row_iota(16, scaled.shape[1])
        scaled = jnp.where(order < fields, scaled, jnp.where(order == fields, w, 0.0))
        hi, lo = split(scaled)
        both = dot(hi, spread[...]) + dot(lo, spread[...])
        mapped_out[...] = both[0:fields] / both[fields : fields + 1]
        keep.wait()

    @pl.when(jnp.logical_not(here))
    def _():
        mapped_out[...] = jnp.zeros(mapped_out.shape, F32)
        senders, slots, block = recv.shape
        fields = arrived.shape[2]
        his = sea.shape[1] // TILE
        flux = jnp.zeros((his * fields, TILE), F32)
        row_b = row_iota(TILE, slots * block).astype(F32).astype(BF16)
        for s in range(senders):
            index = jnp.concatenate([recv[s, k : k + 1, :] for k in range(slots)], axis=1)
            top = index // TILE
            rest = (index - top * TILE).astype(F32).astype(BF16)
            got = jnp.concatenate([arrived[s, k].astype(F32) for k in range(slots)], axis=1)
            parts = [jnp.where(top == h, got, 0.0) for h in range(his)]
            apart = jnp.concatenate(parts, axis=0).astype(BF16)
            flux = flux + dot_nt(apart, one_hot(row_b, rest))
        for h in range(his):
            forcing = exact(force_weight[...], flux[h * fields : (h + 1) * fields])
            at = slice(h * TILE, (h + 1) * TILE)
            sea[:, at] = base[:, at] + forcing
        out = pltpu.make_async_copy(sea, sea_out, sem)
        out.start()
        out.wait()


def vmem():
    return pl.BlockSpec(memory_space=pltpu.VMEM)


def smem():
    return pl.BlockSpec(memory_space=pltpu.SMEM)


def anywhere():
    return pl.BlockSpec(memory_space=pl.ANY)


def on_device(
    atm_state, atm_nbrs, atm_send, atm_mix, flux_weight, margin_counts, margin_weight,
    block_owner, recv_cols, ocn_state, ocn_nbrs, ocn_send, ocn_mix, force_weight, ret_weight,
):
    levels_air, columns = atm_state.shape[2:]
    levels_sea, cells = ocn_state.shape[2:]
    pair = atm_send.shape[2]
    half = pair // 2
    amount_air = atm_nbrs.shape[2]
    amount_sea = ocn_nbrs.shape[2]
    atm_groups, capacity, block = recv_cols.shape[2:]
    row_count = margin_weight.shape[2]
    blocks_here = block_owner.shape[2]
    fields = flux_weight.shape[0]
    ret_fields = ret_weight.shape[0]
    groups = lax.axis_size("grp")
    peers = lax.axis_size("dev")

    air = atm_state.reshape(levels_air, columns)
    sea = ocn_state.reshape(levels_sea, cells)
    counts = margin_counts.reshape(columns // 128, 128)
    weights = margin_weight.reshape(1, row_count)
    owner = block_owner.reshape(1, blocks_here)
    recv = recv_cols.reshape(atm_groups, capacity, block)

    most = max(levels_air, levels_sea)
    params = pltpu.CompilerParams(vmem_limit_bytes=32 * 2**20)
    down, up = pl.pallas_call(
        functools.partial(pack_kernel, atm_groups),
        out_shape=[jax.ShapeDtypeStruct((most, half), BF16)] * 2,
        in_specs=[anywhere(), vmem(), anywhere(), vmem()],
        out_specs=[vmem(), vmem()],
        scratch_shapes=[
            pltpu.VMEM((levels_air, columns), F32),
            pltpu.VMEM((levels_sea, cells), F32),
            pltpu.SemaphoreType.DMA,
        ],
        compiler_params=params,
        name="pack",
    )(air, atm_send.reshape(1, pair), sea, ocn_send.reshape(1, pair))
    higher = [(i, (i + 1) % peers) for i in range(peers)]
    lower = [(j, i) for i, j in higher]
    low = lax.ppermute(up, "dev", higher)
    high = lax.ppermute(down, "dev", lower)

    air_next, base, outgoing = pl.pallas_call(
        functools.partial(mid_kernel, atm_groups),
        out_shape=[
            jax.ShapeDtypeStruct((levels_air, columns), F32),
            jax.ShapeDtypeStruct((levels_sea, cells), F32),
            jax.ShapeDtypeStruct((groups, capacity, fields, block), BF16),
        ],
        in_specs=[
            anywhere(), vmem(), vmem(), vmem(), vmem(), vmem(), smem(), vmem(),
            anywhere(), vmem(), vmem(), vmem(), vmem(), vmem(),
        ],
        out_specs=[anywhere(), vmem(), vmem()],
        scratch_shapes=[
            pltpu.VMEM((levels_air, columns), F32),
            pltpu.VMEM((levels_sea, cells), F32),
            pltpu.VMEM((levels_air, columns + pair), BF16),
            pltpu.VMEM((levels_sea, cells + pair), BF16),
            pltpu.VMEM((row_count, columns), BF16),
            pltpu.VMEM((columns // 128, 128), I32),
            pltpu.VMEM((16 * (cells // TILE), TILE), BF16),
            pltpu.SMEM((groups - atm_groups,), I32),
            pltpu.SemaphoreType.DMA,
            pltpu.SemaphoreType.DMA,
        ],
        compiler_params=params,
        name="mid",
    )(
        air, atm_nbrs.reshape(amount_air, columns), atm_mix.reshape(1, columns), flux_weight,
        counts, weights, owner, recv,
        sea, ocn_nbrs.reshape(amount_sea, 1, cells), ocn_mix.reshape(1, cells), ret_weight,
        low, high,
    )
    arrived = lax.all_to_all(outgoing, "grp", split_axis=0, concat_axis=0, tiled=True)
    sea_next, mapped = pl.pallas_call(
        functools.partial(post_kernel, atm_groups),
        out_shape=[
            jax.ShapeDtypeStruct((levels_sea, cells), F32),
            jax.ShapeDtypeStruct((ret_fields, columns), F32),
        ],
        in_specs=[
            vmem(), vmem(), vmem(), smem(), vmem(), anywhere(), vmem(), vmem(),
        ],
        out_specs=[anywhere(), vmem()],
        scratch_shapes=[
            pltpu.VMEM((levels_sea, cells), F32),
            pltpu.VMEM((row_count, columns), BF16),
            pltpu.VMEM((columns // 128, 128), I32),
            pltpu.VMEM((fields, row_count), F32),
            pltpu.SMEM((groups - atm_groups,), I32),
            pltpu.SemaphoreType.DMA,
        ],
        compiler_params=params,
        name="post",
    )(arrived, counts, weights, owner, recv, sea, base, force_weight)
    return (air_next[None, None], sea_next[None, None], mapped[None, None])


def solution(mesh):
    whole = P("grp", "dev")
    specs = [whole] * 15
    for replicated in (4, 13, 14):
        specs[replicated] = P()
    return jax.shard_map(
        on_device,
        mesh=mesh,
        in_specs=tuple(specs),
        out_specs=(whole, whole, whole),
        check_vma=False,
    )
```

```python
import functools

import jax
import jax.numpy as jnp
from jax import lax
from jax.experimental import pallas as pl
from jax.experimental.pallas import tpu as pltpu
from jax.sharding import PartitionSpec as P

F32 = jnp.float32
BF16 = jnp.bfloat16
I32 = jnp.int32
TILE = 256
NT = (((1,), (1,)), ((), ()))


def dot(a, b):
    return jnp.dot(a, b, preferred_element_type=F32)


def dot_nt(a, b):
    return lax.dot_general(a, b, NT, preferred_element_type=F32)


def split(x):
    hi = x.astype(BF16)
    lo = (x - hi.astype(F32)).astype(BF16)
    return hi, lo


def exact(w, x):
    wh, wl = split(w)
    xh, xl = split(x)
    return dot(wh, xh) + (dot(wl, xh) + dot(wh, xl))


def row_iota(rows, cols):
    return lax.broadcasted_iota(I32, (rows, cols), 0)


def one_hot(rows_bf, index_row):
    return jnp.where(rows_bf == index_row, jnp.ones((), BF16), jnp.zeros((), BF16))


def cast_row(row):
    return row.astype(F32).astype(BF16)


def row_marks(rows, cols):
    return cast_row(row_iota(rows, cols))


def marks_at(picks, base, rows):
    marks = None
    for pick in picks:
        mark = one_hot(rows, cast_row(pick - base))
        marks = mark if marks is None else marks + mark
    return marks


def pack_into(state, send, down, up):
    half = down.shape[1]
    rows = row_marks(TILE, 2 * half)
    index = send[...]
    total = None
    for base in range(0, state.shape[1], TILE):
        part = dot(state[:, base : base + TILE].astype(BF16), marks_at([index], base, rows))
        total = part if total is None else total + part
    out = total.astype(BF16)
    down[...] = out[:, :half]
    up[...] = out[:, half:]


def fetch(source, target, sem):
    copy = pltpu.make_async_copy(source, target, sem)
    copy.start()
    return copy


def fetch_all(pairs, sems):
    return [fetch(source, target, sems.at[i]) for i, (source, target) in enumerate(pairs)]


def wait_all(copies):
    for copy in copies:
        copy.wait()


def air_pack_kernel(atm_groups, air_ref, send_ref, down, up, air, send, sems):
    @pl.when(lax.axis_index("grp") < atm_groups)
    def _():
        wait_all(fetch_all([(send_ref, send), (air_ref, air)], sems))
        pack_into(air, send, down, up)


def own_sums(pool, nbrs, at, width):
    rows = row_marks(TILE, width)
    picks = [n[:, pl.ds(at, width)] for n in nbrs]
    total = None
    for base in range(0, pool.shape[1], TILE):
        part = dot(pool[:, base : base + TILE], marks_at(picks, base, rows))
        total = part if total is None else total + part
    return total


def rim_marks(nbrs, at, width, own):
    picks = [n[:, pl.ds(at, width)] for n in nbrs]
    return marks_at(picks, own, row_marks(TILE, width))


def fill_ends(counts, ends):
    blocks, lanes = counts.shape
    given = cast_row(counts[...])
    upto = jnp.where(
        row_iota(lanes, lanes) <= lax.broadcasted_iota(I32, (lanes, lanes), 1), 1.0, 0.0
    ).astype(BF16)
    within = dot(given, upto)
    whole = dot(given, jnp.ones((lanes, lanes), BF16))
    before = jnp.zeros((1, lanes), F32)
    for j in range(blocks):
        ends[j : j + 1, :] = (within[j : j + 1] + before).astype(I32)
        before = before + whole[j : j + 1]


def fill_spread(counts, ends, spread):
    fill_ends(counts, ends)
    rows, _ = spread.shape
    blocks, lanes = counts.shape
    order = row_iota(rows, lanes)
    for j in range(blocks):
        end = ends[j : j + 1, :]
        begin = end - counts[j : j + 1, :]
        inside = (order >= begin) & (order < end)
        spread[:, j * lanes : (j + 1) * lanes] = jnp.where(inside, 1.0, 0.0).astype(BF16)


def slots_of(owner, seen, visit):
    for o in range(seen.shape[0]):
        seen[o] = 0
    for b in range(owner.shape[1]):
        o = owner[0, b]
        k = seen[o]
        seen[o] = k + 1
        visit(b, o, k)


def look_up(sea, ret_weight, recv, returned, looked):
    cells = sea.shape[1]
    fields = ret_weight.shape[0]
    his = cells // TILE
    pad = returned.shape[0] // his
    for h in range(his):
        chunk = exact(ret_weight[...], sea[:, h * TILE : (h + 1) * TILE])
        chunk = jnp.concatenate([chunk, jnp.zeros((pad - fields, TILE), F32)], axis=0)
        returned[h * pad : (h + 1) * pad, :] = chunk.astype(BF16)
    senders, slots, block = recv.shape
    for s in range(senders):
        index = jnp.concatenate([recv[s, k : k + 1, :] for k in range(slots)], axis=1)
        top = index // TILE
        rest = cast_row(index - top * TILE)
        found = dot(returned[...], one_hot(row_marks(TILE, slots * block), rest))
        look = jnp.zeros((pad, slots * block), F32)
        for h in range(his):
            look = jnp.where(top == h, found[h * pad : (h + 1) * pad], look)
        look = jnp.concatenate(
            [look, jnp.zeros((looked.shape[2] - pad, slots * block), F32)], axis=0
        ).astype(BF16)
        for k in range(slots):
            looked[s, k] = look[:, k * block : (k + 1) * block]


def air_own_kernel(
    atm_groups,
    after, air_ref, air_nbrs_ref, air_mix_ref, counts_ref,
    sea_ref, sea_send_ref, ret_weight_ref, recv_ref,
    part_ref, marks_ref, spread_ref, payload, air_out, sea_down_ref, sea_up_ref,
    air, air_nbrs, air_mix, counts, part, marks, spread, pool, ends,
    sea, sea_send, ret_weight, recv, returned, looked, down, up, sems, out_sems,
):
    here = lax.axis_index("grp") < atm_groups

    @pl.when(here)
    def _():
        near, many, whole, mixed = fetch_all(
            [(air_nbrs_ref, air_nbrs), (counts_ref, counts), (air_ref, air), (air_mix_ref, air_mix)],
            sems,
        )
        amount, columns = air_nbrs.shape
        nbrs = [air_nbrs.at[k : k + 1, :] for k in range(amount)]
        many.wait()
        fill_spread(counts, ends, spread)
        out_spread = fetch(spread, spread_ref, out_sems.at[0])
        near.wait()
        for at in range(0, columns, TILE):
            marks[:, at : at + TILE] = rim_marks(nbrs, at, TILE, columns)
        out_marks = fetch(marks, marks_ref, out_sems.at[1])
        wait_all([whole, mixed])
        pool[...] = air[...].astype(BF16)
        for at in range(0, columns, TILE):
            mix = air_mix[:, at : at + TILE]
            total = own_sums(pool, nbrs, at, TILE)
            own = air[:, at : at + TILE]
            part[:, at : at + TILE] = own + mix * (total * (1.0 / amount) - own)
        out_part = fetch(part, part_ref, out_sems.at[2])
        wait_all([out_spread, out_marks, out_part])

    @pl.when(jnp.logical_not(here))
    def _():
        keep = fetch(air_ref, air_out, out_sems.at[0])
        listed, *rest = fetch_all(
            [
                (sea_send_ref, sea_send),
                (sea_ref, sea),
                (ret_weight_ref, ret_weight),
                (recv_ref, recv),
            ],
            sems,
        )
        wait_all(rest)
        look_up(sea, ret_weight, recv, returned, looked)
        sent = fetch(looked, payload.at[pl.ds(0, atm_groups)], out_sems.at[1])
        listed.wait()
        pack_into(sea, sea_send, down, up)
        out_down = fetch(down, sea_down_ref, out_sems.at[2])
        out_up = fetch(up, sea_up_ref, out_sems.at[3])
        wait_all([sent, out_down, out_up, keep])


def air_send_kernel(
    atm_groups, amount,
    part_ref, marks_ref, spread_ref, low, high, air_mix_ref, flux_weight_ref, weights_ref,
    owner, sea_down_in, sea_up_in, payload_in, air_in,
    payload, air_out, sea_down, sea_up,
    part, marks, spread, air_mix, flux_weight, weights,
    air, rows_out, seen, sems, out_sems,
):
    @pl.when(lax.axis_index("grp") < atm_groups)
    def _():
        last, spreading, *first = fetch_all(
            [
                (weights_ref, weights),
                (spread_ref, spread),
                (marks_ref, marks),
                (part_ref, part),
                (air_mix_ref, air_mix),
                (flux_weight_ref, flux_weight),
            ],
            sems,
        )
        rows_out[...] = jnp.zeros(rows_out.shape, BF16)
        columns = air.shape[1]
        wait_all(first)
        rim = jnp.concatenate([low[...], high[...]], axis=1)
        parts = []
        for at in range(0, columns, TILE):
            total = dot(rim, marks[:, at : at + TILE])
            new = part[:, at : at + TILE] + air_mix[:, at : at + TILE] * (total * (1.0 / amount))
            air[:, at : at + TILE] = new
            parts.append(exact(flux_weight[...], new))
        stored = fetch(air, air_out, out_sems.at[0])
        hi, lo = split(jnp.concatenate(parts, axis=1))
        block = rows_out.shape[3]
        wait_all([last, spreading])

        def visit(b, o, k):
            mark = spread[b * block : (b + 1) * block, :]
            value = dot_nt(hi, mark) + dot_nt(lo, mark)
            value = value * weights[:, b * block : (b + 1) * block]
            rows_out[o, k] = value.astype(BF16)

        slots_of(owner, seen, visit)
        sent = fetch(rows_out, payload.at[pl.ds(atm_groups, rows_out.shape[0])], out_sems.at[1])
        wait_all([stored, sent])


def sea_own_kernel(
    atm_groups,
    after, sea_ref, sea_nbrs_ref,
    sums_ref, marks_ref, sea_out,
    sea, sea_nbrs, sums, marks, pool, sems, out_sems,
):
    here = lax.axis_index("grp") < atm_groups

    @pl.when(here)
    def _():
        fetch(sea_ref, sea_out, out_sems.at[0]).wait()

    @pl.when(jnp.logical_not(here))
    def _():
        near, whole = fetch_all([(sea_nbrs_ref, sea_nbrs), (sea_ref, sea)], sems)
        amount, _, cells = sea_nbrs.shape
        nbrs = [sea_nbrs.at[k] for k in range(amount)]
        near.wait()
        for at in range(0, cells, TILE):
            marks[:, at : at + TILE] = rim_marks(nbrs, at, TILE, cells)
        out_marks = fetch(marks, marks_ref, out_sems.at[1])
        whole.wait()
        pool[...] = sea[...].astype(BF16)

        def step(i, carry):
            at = pl.multiple_of(i * TILE, TILE)
            sums[:, pl.ds(at, TILE)] = own_sums(pool, nbrs, at, TILE)
            return carry

        lax.fori_loop(0, cells // TILE, step, 0)
        out_sums = fetch(sums, sums_ref, out_sems.at[0])
        wait_all([out_marks, out_sums])


def last_kernel(
    atm_groups, amount,
    arrived, spread_ref, weights_ref, owner,
    recv_ref, sea_ref, sums_ref, marks_ref, low, high, sea_mix_ref, force_weight_ref, sea_in,
    sea_out, mapped_ref,
    spread, weights, mine, mapped, seen,
    recv, sea, sums, marks, sea_mix, force_weight, sems, out_sems,
):
    here = lax.axis_index("grp") < atm_groups
    fields, _, columns = mapped.shape

    @pl.when(here)
    def _():
        given, spreading = fetch_all([(weights_ref, weights), (spread_ref, spread)], sems)
        block = arrived.shape[3]
        given.wait()

        def visit(b, o, k):
            mine[:, b * block : (b + 1) * block] = arrived[atm_groups + o, k].astype(F32)

        slots_of(owner, seen, visit)
        w = weights[...]
        scaled = mine[0:16, :] * w
        order = row_iota(16, scaled.shape[1])
        scaled = jnp.where(order < fields, scaled, jnp.where(order == fields, w, 0.0))
        hi, lo = split(scaled)
        spreading.wait()
        both = dot(hi, spread[...]) + dot(lo, spread[...])
        mean = both[0:fields] / both[fields : fields + 1]
        for f in range(fields):
            mapped[f] = mean[f : f + 1]
        fetch(mapped, mapped_ref, out_sems.at[0]).wait()

    @pl.when(jnp.logical_not(here))
    def _():
        mapped[...] = jnp.zeros(mapped.shape, F32)
        stored = fetch(mapped, mapped_ref, out_sems.at[0])
        cells_in, *rest = fetch_all(
            [
                (recv_ref, recv),
                (sea_ref, sea),
                (sums_ref, sums),
                (marks_ref, marks),
                (sea_mix_ref, sea_mix),
                (force_weight_ref, force_weight),
            ],
            sems,
        )
        senders, slots, block = recv.shape
        rows = arrived.shape[2]
        his = sea.shape[1] // TILE
        flux = jnp.zeros((his * rows, TILE), F32)
        cells_in.wait()
        for s in range(senders):
            index = jnp.concatenate([recv[s, k : k + 1, :] for k in range(slots)], axis=1)
            top = index // TILE
            rest_of = cast_row(index - top * TILE)
            values = jnp.concatenate([arrived[s, k].astype(F32) for k in range(slots)], axis=1)
            parts = [jnp.where(top == h, values, 0.0) for h in range(his)]
            apart = jnp.concatenate(parts, axis=0).astype(BF16)
            flux = flux + dot_nt(apart, one_hot(row_marks(TILE, slots * block), rest_of))
        wait_all(rest)
        rim = jnp.concatenate([low[...], high[...]], axis=1)
        for h in range(his):
            at = slice(h * TILE, (h + 1) * TILE)
            forcing = exact(force_weight[...], flux[h * rows : (h + 1) * rows])
            total = sums[:, at] + dot(rim, marks[:, at])
            own = sea[:, at]
            sea[:, at] = own + sea_mix[:, at] * (total * (1.0 / amount) - own) + forcing
        out = fetch(sea, sea_out, out_sems.at[1])
        wait_all([stored, out])


def vmem():
    return pl.BlockSpec(memory_space=pltpu.VMEM)


def smem():
    return pl.BlockSpec(memory_space=pltpu.SMEM)


def anywhere():
    return pl.BlockSpec(memory_space=pl.ANY)


def in_hbm(x):
    return pltpu.with_memory_space_constraint(x, pltpu.HBM)


def shape(dims, dtype):
    return jax.ShapeDtypeStruct(dims, dtype)


def on_device(
    atm_state, atm_nbrs, atm_send, atm_mix, flux_weight, margin_counts, margin_weight,
    block_owner, recv_cols, ocn_state, ocn_nbrs, ocn_send, ocn_mix, force_weight, ret_weight,
):
    levels_air, columns = atm_state.shape[2:]
    levels_sea, cells = ocn_state.shape[2:]
    pair = atm_send.shape[2]
    half = pair // 2
    amount_air = atm_nbrs.shape[2]
    amount_sea = ocn_nbrs.shape[2]
    atm_groups, capacity, block = recv_cols.shape[2:]
    row_count = margin_weight.shape[2]
    blocks_here = block_owner.shape[2]
    fields = flux_weight.shape[0]
    ret_fields = ret_weight.shape[0]
    groups = lax.axis_size("grp")
    peers = lax.axis_size("dev")

    air = atm_state.reshape(levels_air, columns)
    sea = ocn_state.reshape(levels_sea, cells)
    counts = margin_counts.reshape(columns // 128, 128)
    weights = margin_weight.reshape(1, row_count)
    owner = block_owner.reshape(1, blocks_here)
    recv = recv_cols.reshape(atm_groups, capacity, block)
    air_mix = atm_mix.reshape(1, columns)
    air_shape = shape((levels_air, columns), F32)
    sea_shape = shape((levels_sea, cells), F32)
    air_rim = shape((levels_air, half), BF16)
    sea_rim = shape((levels_sea, half), BF16)
    payload_shape = shape((groups, capacity, fields, block), BF16)
    sent_shape = (capacity, fields, block)
    dma = pltpu.SemaphoreType.DMA

    def scratch(*dims, dtype=F32):
        return pltpu.VMEM(dims, dtype)

    air_scratch = scratch(levels_air, columns)
    sea_scratch = scratch(levels_sea, cells)
    air_marks = scratch(pair, columns, dtype=BF16)
    sea_marks_in = scratch(pair, cells, dtype=BF16)
    spread_in = scratch(row_count, columns, dtype=BF16)
    sea_half = scratch(levels_sea, half, dtype=BF16)
    pair_in = scratch(1, pair, dtype=I32)
    recv_in = scratch(atm_groups, capacity, block, dtype=I32)
    weights_in = scratch(1, row_count)
    air_row = scratch(1, columns)
    params = pltpu.CompilerParams(vmem_limit_bytes=60 * 2**20)

    def shifted(value, first, last, step):
        line = [
            (g * peers + i, g * peers + (i + step) % peers)
            for g in range(first, last)
            for i in range(peers)
        ]
        return in_hbm(lax.ppermute(value, ("grp", "dev"), line))

    down, up = pl.pallas_call(
        functools.partial(air_pack_kernel, atm_groups),
        out_shape=[air_rim] * 2,
        in_specs=[anywhere()] * 2,
        out_specs=[vmem(), vmem()],
        scratch_shapes=[air_scratch, pair_in, dma((2,))],
        compiler_params=params,
        name="air_pack",
    )(air, atm_send.reshape(1, pair))
    low = shifted(up, 0, atm_groups, 1)
    high = shifted(down, 0, atm_groups, -1)

    part, marks, spread, payload, air_pre, sea_down, sea_up = pl.pallas_call(
        functools.partial(air_own_kernel, atm_groups),
        out_shape=[
            air_shape,
            shape((pair, columns), BF16),
            shape((row_count, columns), BF16),
            payload_shape,
            air_shape,
            sea_rim,
            sea_rim,
        ],
        in_specs=[anywhere()] * 9,
        out_specs=[anywhere()] * 7,
        scratch_shapes=[
            air_scratch,
            scratch(amount_air, columns, dtype=I32),
            air_row,
            scratch(columns // 128, 128, dtype=I32),
            air_scratch,
            air_marks,
            spread_in,
            scratch(levels_air, columns, dtype=BF16),
            scratch(columns // 128, 128, dtype=I32),
            sea_scratch,
            pair_in,
            scratch(ret_fields, levels_sea),
            recv_in,
            scratch(16 * (cells // TILE), TILE, dtype=BF16),
            scratch(atm_groups, *sent_shape, dtype=BF16),
            sea_half,
            sea_half,
            dma((4,)),
            dma((4,)),
        ],
        compiler_params=params,
        cost_estimate=pl.CostEstimate(flops=4 * 10**9, bytes_accessed=10**7, transcendentals=0),
        name="air_own",
    )(
        up, air, atm_nbrs.reshape(amount_air, columns), air_mix, counts,
        sea, ocn_send.reshape(1, pair), ret_weight, recv,
    )
    payload, air_next, sea_down, sea_up = pl.pallas_call(
        functools.partial(air_send_kernel, atm_groups, amount_air),
        out_shape=[payload_shape, air_shape, sea_rim, sea_rim],
        in_specs=[anywhere()] * 3 + [vmem()] * 2 + [anywhere()] * 3 + [smem()] + [anywhere()] * 4,
        out_specs=[anywhere()] * 4,
        scratch_shapes=[
            air_scratch,
            air_marks,
            spread_in,
            air_row,
            scratch(fields, levels_air),
            weights_in,
            air_scratch,
            scratch(groups - atm_groups, *sent_shape, dtype=BF16),
            pltpu.SMEM((groups - atm_groups,), I32),
            dma((6,)),
            dma((2,)),
        ],
        input_output_aliases={11: 0, 12: 1, 9: 2, 10: 3},
        compiler_params=params,
        name="air_send",
    )(
        part, marks, spread, low, high, air_mix, flux_weight, weights, owner,
        sea_down, sea_up, payload, air_pre,
    )
    arrived = in_hbm(lax.all_to_all(payload, "grp", split_axis=0, concat_axis=0, tiled=True))
    sea_low = shifted(sea_up, atm_groups, groups, 1)
    sea_high = shifted(sea_down, atm_groups, groups, -1)

    sums, sea_marks, sea_pre = pl.pallas_call(
        functools.partial(sea_own_kernel, atm_groups),
        out_shape=[sea_shape, shape((pair, cells), BF16), sea_shape],
        in_specs=[anywhere()] * 3,
        out_specs=[anywhere()] * 3,
        scratch_shapes=[
            sea_scratch,
            scratch(amount_sea, 1, cells, dtype=I32),
            sea_scratch,
            sea_marks_in,
            scratch(levels_sea, cells, dtype=BF16),
            dma((2,)),
            dma((2,)),
        ],
        compiler_params=params,
        cost_estimate=pl.CostEstimate(flops=8 * 10**9, bytes_accessed=10**7, transcendentals=0),
        name="sea_own",
    )(payload, sea, ocn_nbrs.reshape(amount_sea, 1, cells))
    sea_next, mapped = pl.pallas_call(
        functools.partial(last_kernel, atm_groups, amount_sea),
        out_shape=[sea_shape, shape((ret_fields, 1, columns), F32)],
        in_specs=[vmem()] + [anywhere()] * 2 + [smem()] + [anywhere()] * 4 + [vmem()] * 2 + [anywhere()] * 3,
        out_specs=[anywhere()] * 2,
        scratch_shapes=[
            spread_in,
            weights_in,
            scratch(fields, row_count),
            scratch(ret_fields, 1, columns),
            pltpu.SMEM((groups - atm_groups,), I32),
            recv_in,
            sea_scratch,
            sea_scratch,
            sea_marks_in,
            scratch(1, cells),
            scratch(levels_sea, fields),
            dma((6,)),
            dma((2,)),
        ],
        input_output_aliases={12: 0},
        compiler_params=params,
        name="last",
    )(
        arrived, spread, weights, owner,
        recv, sea, sums, sea_marks, sea_low, sea_high, ocn_mix.reshape(1, cells), force_weight,
        sea_pre,
    )
    mapped = mapped.reshape(1, 1, ret_fields, columns)
    return (air_next[None, None], sea_next[None, None], mapped)


def solution(mesh):
    whole = P("grp", "dev")
    specs = [whole] * 15
    for replicated in (4, 13, 14):
        specs[replicated] = P()
    return jax.shard_map(
        on_device,
        mesh=mesh,
        in_specs=tuple(specs),
        out_specs=(whole, whole, whole),
        check_vma=False,
    )
```

```python
import functools

import jax
import jax.numpy as jnp
from jax import lax
from jax.experimental import pallas as pl
from jax.experimental.pallas import tpu as pltpu
from jax.sharding import PartitionSpec as P

F32 = jnp.float32
BF16 = jnp.bfloat16
I32 = jnp.int32
I16 = jnp.int16
TILE = 256
NT = (((1,), (1,)), ((), ()))


def dot(a, b):
    return jnp.dot(a, b, preferred_element_type=F32)


def dot_nt(a, b):
    return lax.dot_general(a, b, NT, preferred_element_type=F32)


def split(x):
    hi = x.astype(BF16)
    lo = (x - hi.astype(F32)).astype(BF16)
    return hi, lo


def exact(w, x):
    wh, wl = split(w)
    xh, xl = split(x)
    return dot(wh, xh) + (dot(wl, xh) + dot(wh, xl))


def row_iota(rows, cols):
    return lax.broadcasted_iota(I32, (rows, cols), 0)


def one_hot(rows_bf, index_row):
    return jnp.where(rows_bf == index_row, jnp.ones((), BF16), jnp.zeros((), BF16))


def cast_row(row):
    return row.astype(F32).astype(BF16)


def row_marks(rows, cols):
    return cast_row(row_iota(rows, cols))


def marks_at(picks, base, rows):
    marks = None
    for pick in picks:
        mark = one_hot(rows, cast_row(pick - base))
        marks = mark if marks is None else marks + mark
    return marks


def pack_into(state, send, down, up):
    half = down.shape[1]
    rows = row_marks(TILE, 2 * half)
    index = send[...]
    total = None
    for base in range(0, state.shape[1], TILE):
        part = dot(state[:, base : base + TILE].astype(BF16), marks_at([index], base, rows))
        total = part if total is None else total + part
    out = total.astype(BF16)
    down[...] = out[:, :half]
    up[...] = out[:, half:]


def fetch(source, target, sem):
    copy = pltpu.make_async_copy(source, target, sem)
    copy.start()
    return copy


def fetch_all(pairs, sems):
    return [fetch(source, target, sems.at[i]) for i, (source, target) in enumerate(pairs)]


def wait_all(copies):
    for copy in copies:
        copy.wait()


def air_pack_kernel(atm_groups, air_ref, send_ref, down, up, air, send, sems):
    @pl.when(lax.axis_index("grp") < atm_groups)
    def _():
        wait_all(fetch_all([(send_ref, send), (air_ref, air)], sems))
        pack_into(air, send, down, up)


def sums_of(pool, nbrs, at, width):
    rows = row_marks(TILE, width)
    picks = [n[:, pl.ds(at, width)] for n in nbrs]
    total = None
    for base in range(0, pool.shape[1], TILE):
        part = dot(pool[:, base : base + TILE], marks_at(picks, base, rows))
        total = part if total is None else total + part
    return total


def rim_marks(nbrs, at, width, own):
    picks = [n[:, pl.ds(at, width)] for n in nbrs]
    return marks_at(picks, own, row_marks(TILE, width))


def fill_ends(counts, ends):
    blocks, lanes = counts.shape
    given = cast_row(counts[...])
    upto = jnp.where(
        row_iota(lanes, lanes) <= lax.broadcasted_iota(I32, (lanes, lanes), 1), 1.0, 0.0
    ).astype(BF16)
    within = dot(given, upto)
    whole = dot(given, jnp.ones((lanes, lanes), BF16))
    before = jnp.zeros((1, lanes), F32)
    for j in range(blocks):
        ends[j : j + 1, :] = (within[j : j + 1] + before).astype(I32)
        before = before + whole[j : j + 1]


def interval(order, begin, end):
    return jnp.where((order >= begin) & (order < end), jnp.ones((), BF16), jnp.zeros((), BF16))


def fill_limits(counts, ends, begins_at, ends_at):
    blocks, lanes = counts.shape
    end = jnp.transpose(ends[...].astype(F32)).astype(I32)
    begin = jnp.transpose((ends[...] - counts[...]).astype(F32)).astype(I32)
    for j in range(blocks):
        at = slice(j * lanes, (j + 1) * lanes)
        ends_at[at, :] = jnp.broadcast_to(end[:, j : j + 1], (lanes, lanes)).astype(I16)
        begins_at[at, :] = jnp.broadcast_to(begin[:, j : j + 1], (lanes, lanes)).astype(I16)


def spread_rows(values, begins_at, ends_at, tile):
    columns, lanes = ends_at.shape
    reach = (columns // 2) // TILE
    lane = lax.broadcasted_iota(I32, (TILE, lanes), 1)
    total = None
    for t in range(max(0, tile - reach), min(tile, columns // TILE - 1) + 1):
        at = slice(t * TILE, (t + 1) * TILE)
        sides = []
        for side in range(TILE // lanes):
            order = (lane + (tile * TILE + side * lanes)).astype(I16)
            sides.append(interval(order, begins_at[at, :], ends_at[at, :]))
        part = dot(values[:, at], jnp.concatenate(sides, axis=1))
        total = part if total is None else total + part
    return total


def gather_rows(values, counts, ends, tile):
    blocks, lanes = counts.shape
    reach = (blocks * lanes // 2) // TILE
    each = TILE // lanes
    end = jnp.concatenate([ends[tile * each + i : tile * each + i + 1, :] for i in range(each)], axis=1)
    count = jnp.concatenate(
        [counts[tile * each + i : tile * each + i + 1, :] for i in range(each)], axis=1
    )
    begin = (end - count).astype(I16)
    end = end.astype(I16)
    rows = row_iota(TILE, TILE)
    total = None
    for t in range(tile, tile + reach + 1):
        mark = interval((rows + t * TILE).astype(I16), begin, end)
        part = dot(values[:, t * TILE : (t + 1) * TILE], mark)
        total = part if total is None else total + part
    return total


def slots_of(owner, seen, visit):
    for o in range(seen.shape[0]):
        seen[o] = 0
    for b in range(owner.shape[1]):
        o = owner[0, b]
        k = seen[o]
        seen[o] = k + 1
        visit(b, o, k)


def look_up(sea, ret_weight, recv, returned, looked):
    cells = sea.shape[1]
    fields = ret_weight.shape[0]
    his = cells // TILE
    pad = returned.shape[0] // his
    for h in range(his):
        chunk = exact(ret_weight[...], sea[:, h * TILE : (h + 1) * TILE])
        chunk = jnp.concatenate([chunk, jnp.zeros((pad - fields, TILE), F32)], axis=0)
        returned[h * pad : (h + 1) * pad, :] = chunk.astype(BF16)
    senders, slots, block = recv.shape
    for s in range(senders):
        index = jnp.concatenate([recv[s, k : k + 1, :] for k in range(slots)], axis=1)
        top = index // TILE
        rest = cast_row(index - top * TILE)
        found = dot(returned[...], one_hot(row_marks(TILE, slots * block), rest))
        look = jnp.zeros((pad, slots * block), F32)
        for h in range(his):
            look = jnp.where(top == h, found[h * pad : (h + 1) * pad], look)
        look = jnp.concatenate(
            [look, jnp.zeros((looked.shape[2] - pad, slots * block), F32)], axis=0
        ).astype(BF16)
        for k in range(slots):
            looked[s, k] = look[:, k * block : (k + 1) * block]


def mid_kernel(
    atm_groups,
    low, high, air_ref, air_nbrs_ref, air_mix_ref, counts_ref, flux_weight_ref, weights_ref, owner,
    sea_ref, sea_send_ref, ret_weight_ref, recv_ref,
    payload, air_out, sea_down_ref, sea_up_ref,
    air, air_nbrs, air_mix, counts, flux_weight, weights,
    pool, ends, begins_at, ends_at, values, sent, seen,
    sea, sea_send, ret_weight, recv, returned, down, up, sems, out_sems,
):
    here = lax.axis_index("grp") < atm_groups
    count_groups = sent.shape[0]

    @pl.when(here)
    def _():
        many, near, whole, mixed, *rest = fetch_all(
            [
                (counts_ref, counts),
                (air_nbrs_ref, air_nbrs),
                (air_ref, air),
                (air_mix_ref, air_mix),
                (flux_weight_ref, flux_weight),
                (weights_ref, weights),
            ],
            sems,
        )
        sent[...] = jnp.zeros(sent.shape, BF16)
        values[...] = jnp.zeros(values.shape, BF16)
        many.wait()
        fill_ends(counts, ends)
        fill_limits(counts, ends, begins_at, ends_at)
        amount, columns = air_nbrs.shape
        half = low.shape[1]
        pool[:, columns : columns + half] = low[...]
        pool[:, columns + half :] = high[...]
        wait_all([near, whole, mixed, *rest])
        pool[:, :columns] = air[...].astype(BF16)
        nbrs = [air_nbrs.at[k : k + 1, :] for k in range(amount)]
        fields = flux_weight.shape[0]
        for at in range(0, columns, TILE):
            total = sums_of(pool, nbrs, at, TILE)
            own = air[:, at : at + TILE]
            new = own + air_mix[:, at : at + TILE] * (total * (1.0 / amount) - own)
            air[:, at : at + TILE] = new
            hi, lo = split(exact(flux_weight[...], new))
            values[0:fields, at : at + TILE] = hi
            values[32 : 32 + fields, at : at + TILE] = lo
        stored = fetch(air, air_out, out_sems.at[0])
        block = sent.shape[3]
        each = TILE // block
        tiles = []
        for t in range(weights.shape[1] // TILE):
            both = spread_rows(values, begins_at, ends_at, t)
            tile = (both[0:fields] + both[32 : 32 + fields]) * weights[:, t * TILE : (t + 1) * TILE]
            tiles.append(tile.astype(BF16))

        def visit(b, o, k):
            i = b % each
            sent[o, k] = tiles[b // each][:, i * block : (i + 1) * block]

        slots_of(owner, seen, visit)
        done = fetch(sent, payload.at[pl.ds(atm_groups, count_groups)], out_sems.at[1])
        wait_all([stored, done])

    @pl.when(jnp.logical_not(here))
    def _():
        listed, kept, *rest = fetch_all(
            [
                (sea_send_ref, sea_send),
                (air_ref, air),
                (sea_ref, sea),
                (ret_weight_ref, ret_weight),
                (recv_ref, recv),
            ],
            sems,
        )
        wait_all(rest)
        look_up(sea, ret_weight, recv, returned, sent)
        done = fetch(sent, payload.at[pl.ds(0, atm_groups)], out_sems.at[1])
        kept.wait()
        keep = fetch(air, air_out, out_sems.at[0])
        listed.wait()
        pack_into(sea, sea_send, down, up)
        out_down = fetch(down, sea_down_ref, out_sems.at[2])
        out_up = fetch(up, sea_up_ref, out_sems.at[3])
        wait_all([done, keep, out_down, out_up])


def sea_own_kernel(
    atm_groups,
    after, sea_ref, sea_nbrs_ref,
    sums_ref, marks_ref, sea_out,
    sea, sea_nbrs, sums, marks, pool, sems, out_sems,
):
    here = lax.axis_index("grp") < atm_groups

    @pl.when(here)
    def _():
        fetch(sea_ref, sea, sems.at[0]).wait()
        fetch(sea, sea_out, out_sems.at[0]).wait()

    @pl.when(jnp.logical_not(here))
    def _():
        near, whole = fetch_all([(sea_nbrs_ref, sea_nbrs), (sea_ref, sea)], sems)
        amount, _, cells = sea_nbrs.shape
        nbrs = [sea_nbrs.at[k] for k in range(amount)]
        near.wait()
        for at in range(0, cells, TILE):
            marks[:, at : at + TILE] = rim_marks(nbrs, at, TILE, cells)
        out_marks = fetch(marks, marks_ref, out_sems.at[1])
        whole.wait()
        pool[...] = sea[...].astype(BF16)

        def step(i, carry):
            at = pl.multiple_of(i * TILE, TILE)
            sums[:, pl.ds(at, TILE)] = sums_of(pool, nbrs, at, TILE)
            return carry

        lax.fori_loop(0, cells // TILE, step, 0)
        out_sums = fetch(sums, sums_ref, out_sems.at[0])
        wait_all([out_marks, out_sums])


def last_kernel(
    atm_groups, amount,
    arrived, counts_ref, weights_ref, owner,
    recv_ref, sea_ref, sums_ref, marks_ref, low, high, sea_mix_ref, force_weight_ref, sea_in,
    sea_out, mapped_ref,
    counts, ends, weights, mine, mapped, seen,
    recv, sea, sums, marks, sea_mix, force_weight, sems, out_sems,
):
    here = lax.axis_index("grp") < atm_groups
    fields, _, columns = mapped.shape

    @pl.when(here)
    def _():
        many, given = fetch_all([(counts_ref, counts), (weights_ref, weights)], sems)
        block = arrived.shape[3]

        def visit(b, o, k):
            mine[:, b * block : (b + 1) * block] = arrived[atm_groups + o, k].astype(F32)

        slots_of(owner, seen, visit)
        many.wait()
        fill_ends(counts, ends)
        given.wait()
        w = weights[...]
        scaled = mine[0:16, :] * w
        order = row_iota(16, scaled.shape[1])
        scaled = jnp.where(order < fields, scaled, jnp.where(order == fields, w, 0.0))
        hi, lo = split(scaled)
        both_in = jnp.concatenate([hi, lo], axis=0)
        for t in range(columns // TILE):
            both = gather_rows(both_in, counts, ends, t)
            both = both[0:16] + both[16:32]
            mean = both[0:fields] / both[fields : fields + 1]
            for f in range(fields):
                mapped[f, :, t * TILE : (t + 1) * TILE] = mean[f : f + 1]
        fetch(mapped, mapped_ref, out_sems.at[0]).wait()

    @pl.when(jnp.logical_not(here))
    def _():
        mapped[...] = jnp.zeros(mapped.shape, F32)
        stored = fetch(mapped, mapped_ref, out_sems.at[0])
        cells_in, *rest = fetch_all(
            [
                (recv_ref, recv),
                (sea_ref, sea),
                (sums_ref, sums),
                (marks_ref, marks),
                (sea_mix_ref, sea_mix),
                (force_weight_ref, force_weight),
            ],
            sems,
        )
        senders, slots, block = recv.shape
        rows = arrived.shape[2]
        his = sea.shape[1] // TILE
        flux = jnp.zeros((his * rows, TILE), F32)
        cells_in.wait()
        for s in range(senders):
            index = jnp.concatenate([recv[s, k : k + 1, :] for k in range(slots)], axis=1)
            top = index // TILE
            rest_of = cast_row(index - top * TILE)
            values = jnp.concatenate([arrived[s, k].astype(F32) for k in range(slots)], axis=1)
            parts = [jnp.where(top == h, values, 0.0) for h in range(his)]
            apart = jnp.concatenate(parts, axis=0).astype(BF16)
            flux = flux + dot_nt(apart, one_hot(row_marks(TILE, slots * block), rest_of))
        wait_all(rest)
        rim = jnp.concatenate([low[...], high[...]], axis=1)
        spread_weight = jnp.transpose(force_weight[...])
        for h in range(his):
            at = slice(h * TILE, (h + 1) * TILE)
            forcing = exact(spread_weight, flux[h * rows : (h + 1) * rows])
            total = sums[:, at] + dot(rim, marks[:, at])
            own = sea[:, at]
            sea[:, at] = own + sea_mix[:, at] * (total * (1.0 / amount) - own) + forcing
        out = fetch(sea, sea_out, out_sems.at[1])
        wait_all([stored, out])


def vmem():
    return pl.BlockSpec(memory_space=pltpu.VMEM)


def smem():
    return pl.BlockSpec(memory_space=pltpu.SMEM)


def anywhere():
    return pl.BlockSpec(memory_space=pl.ANY)


def in_hbm(x):
    return pltpu.with_memory_space_constraint(x, pltpu.HBM)


def shape(dims, dtype):
    return jax.ShapeDtypeStruct(dims, dtype)


def on_device(
    atm_state, atm_nbrs, atm_send, atm_mix, flux_weight, margin_counts, margin_weight,
    block_owner, recv_cols, ocn_state, ocn_nbrs, ocn_send, ocn_mix, force_weight, ret_weight,
):
    levels_air, columns = atm_state.shape[2:]
    levels_sea, cells = ocn_state.shape[2:]
    pair = atm_send.shape[2]
    half = pair // 2
    amount_air = atm_nbrs.shape[2]
    amount_sea = ocn_nbrs.shape[2]
    atm_groups, capacity, block = recv_cols.shape[2:]
    row_count = margin_weight.shape[2]
    blocks_here = block_owner.shape[2]
    fields = flux_weight.shape[0]
    ret_fields = ret_weight.shape[0]
    groups = lax.axis_size("grp")
    peers = lax.axis_size("dev")

    air = in_hbm(atm_state.reshape(levels_air, columns))
    sea = in_hbm(ocn_state.reshape(levels_sea, cells))
    counts = in_hbm(margin_counts.reshape(columns // 128, 128))
    weights = in_hbm(margin_weight.reshape(1, row_count))
    owner = in_hbm(block_owner.reshape(1, blocks_here))
    recv = in_hbm(recv_cols.reshape(atm_groups, capacity, block))
    air_mix = in_hbm(atm_mix.reshape(1, columns))
    air_shape = shape((levels_air, columns), F32)
    sea_shape = shape((levels_sea, cells), F32)
    air_rim = shape((levels_air, half), BF16)
    sea_rim = shape((levels_sea, half), BF16)
    payload_shape = shape((groups, capacity, fields, block), BF16)
    sent_shape = (capacity, fields, block)
    dma = pltpu.SemaphoreType.DMA

    def scratch(*dims, dtype=F32):
        return pltpu.VMEM(dims, dtype)

    air_scratch = scratch(levels_air, columns)
    sea_scratch = scratch(levels_sea, cells)
    sea_marks_in = scratch(pair, cells, dtype=BF16)
    counts_in = scratch(columns // 128, 128, dtype=I32)
    sea_half = scratch(levels_sea, half, dtype=BF16)
    pair_in = scratch(1, pair, dtype=I32)
    recv_in = scratch(atm_groups, capacity, block, dtype=I32)
    weights_in = scratch(1, row_count)
    air_row = scratch(1, columns)
    params = pltpu.CompilerParams(vmem_limit_bytes=24 * 2**20)

    def shifted(value, first, last, step):
        line = [
            (g * peers + i, g * peers + (i + step) % peers)
            for g in range(first, last)
            for i in range(peers)
        ]
        return lax.ppermute(value, ("grp", "dev"), line)

    down, up = pl.pallas_call(
        functools.partial(air_pack_kernel, atm_groups),
        out_shape=[air_rim] * 2,
        in_specs=[anywhere()] * 2,
        out_specs=[vmem(), vmem()],
        scratch_shapes=[air_scratch, pair_in, dma((2,))],
        compiler_params=params,
        name="air_pack",
    )(air, in_hbm(atm_send.reshape(1, pair)))
    low = shifted(up, 0, atm_groups, 1)
    high = shifted(down, 0, atm_groups, -1)

    payload, air_next, sea_down, sea_up = pl.pallas_call(
        functools.partial(mid_kernel, atm_groups),
        out_shape=[payload_shape, air_shape, sea_rim, sea_rim],
        in_specs=[vmem()] * 2 + [anywhere()] * 6 + [smem()] + [anywhere()] * 4,
        out_specs=[anywhere()] * 4,
        scratch_shapes=[
            air_scratch,
            scratch(amount_air, columns, dtype=I32),
            air_row,
            counts_in,
            scratch(fields, levels_air),
            weights_in,
            scratch(levels_air, columns + pair, dtype=BF16),
            counts_in,
            scratch(columns, 128, dtype=I16),
            scratch(columns, 128, dtype=I16),
            scratch(64, columns, dtype=BF16),
            scratch(atm_groups, *sent_shape, dtype=BF16),
            pltpu.SMEM((groups - atm_groups,), I32),
            sea_scratch,
            pair_in,
            scratch(ret_fields, levels_sea),
            recv_in,
            scratch(16 * (cells // TILE), TILE, dtype=BF16),
            sea_half,
            sea_half,
            dma((6,)),
            dma((4,)),
        ],
        compiler_params=params,
        name="mid",
    )(
        low, high, air, in_hbm(atm_nbrs.reshape(amount_air, columns)), air_mix, counts, in_hbm(flux_weight),
        weights, owner, sea, in_hbm(ocn_send.reshape(1, pair)), in_hbm(ret_weight), recv,
    )
    arrived = lax.all_to_all(payload, "grp", split_axis=0, concat_axis=0, tiled=True)
    sea_low = shifted(sea_up, atm_groups, groups, 1)
    sea_high = shifted(sea_down, atm_groups, groups, -1)

    sums, sea_marks, sea_pre = pl.pallas_call(
        functools.partial(sea_own_kernel, atm_groups),
        out_shape=[sea_shape, shape((pair, cells), BF16), sea_shape],
        in_specs=[anywhere()] * 3,
        out_specs=[anywhere()] * 3,
        scratch_shapes=[
            sea_scratch,
            scratch(amount_sea, 1, cells, dtype=I32),
            sea_scratch,
            sea_marks_in,
            scratch(levels_sea, cells, dtype=BF16),
            dma((2,)),
            dma((2,)),
        ],
        compiler_params=params,
        cost_estimate=pl.CostEstimate(flops=8 * 10**9, bytes_accessed=10**7, transcendentals=0),
        name="sea_own",
    )(payload, sea, in_hbm(ocn_nbrs.reshape(amount_sea, 1, cells)))
    sea_next, mapped = pl.pallas_call(
        functools.partial(last_kernel, atm_groups, amount_sea),
        out_shape=[sea_shape, shape((ret_fields, 1, columns), F32)],
        in_specs=[vmem()] + [anywhere()] * 2 + [smem()] + [anywhere()] * 4 + [vmem()] * 2 + [anywhere()] * 3,
        out_specs=[anywhere()] * 2,
        scratch_shapes=[
            counts_in,
            counts_in,
            weights_in,
            scratch(fields, row_count),
            scratch(ret_fields, 1, columns),
            pltpu.SMEM((groups - atm_groups,), I32),
            recv_in,
            sea_scratch,
            sea_scratch,
            sea_marks_in,
            scratch(1, cells),
            scratch(fields, levels_sea),
            dma((6,)),
            dma((2,)),
        ],
        input_output_aliases={12: 0},
        compiler_params=params,
        name="last",
    )(
        arrived, counts, weights, owner,
        recv, sea, sums, sea_marks, sea_low, sea_high, in_hbm(ocn_mix.reshape(1, cells)), in_hbm(force_weight.T),
        sea_pre,
    )
    mapped = mapped.reshape(1, 1, ret_fields, columns)
    return (air_next[None, None], sea_next[None, None], mapped)


def solution(mesh):
    whole = P("grp", "dev")
    specs = [whole] * 15
    for replicated in (4, 13, 14):
        specs[replicated] = P()
    return jax.shard_map(
        on_device,
        mesh=mesh,
        in_specs=tuple(specs),
        out_specs=(whole, whole, whole),
        check_vma=False,
    )
```

```python
import functools

import jax
import jax.numpy as jnp
from jax import lax
from jax.experimental import pallas as pl
from jax.experimental.pallas import tpu as pltpu
from jax.sharding import PartitionSpec as P

F32 = jnp.float32
BF16 = jnp.bfloat16
I32 = jnp.int32
I16 = jnp.int16
TILE = 256
NT = (((1,), (1,)), ((), ()))


def dot(a, b):
    return jnp.dot(a, b, preferred_element_type=F32)


def dot_nt(a, b):
    return lax.dot_general(a, b, NT, preferred_element_type=F32)


def split(x):
    hi = x.astype(BF16)
    lo = (x - hi.astype(F32)).astype(BF16)
    return hi, lo


def exact(w, x):
    wh, wl = split(w)
    xh, xl = split(x)
    return dot(wh, xh) + (dot(wl, xh) + dot(wh, xl))


def row_iota(rows, cols):
    return lax.broadcasted_iota(I32, (rows, cols), 0)


def one_hot(rows_bf, index_row):
    return jnp.where(rows_bf == index_row, jnp.ones((), BF16), jnp.zeros((), BF16))


def cast_row(row):
    return row.astype(F32).astype(BF16)


def row_marks(rows, cols):
    return cast_row(row_iota(rows, cols))


def marks_at(picks, base, rows):
    marks = None
    for pick in picks:
        mark = one_hot(rows, cast_row(pick - base))
        marks = mark if marks is None else marks + mark
    return marks


def is_even():
    return lax.rem(lax.axis_index("dev"), 2) == 0


def pack_into(state, send, first, second):
    half = first.shape[1]
    rows = row_marks(TILE, 2 * half)
    index = send[...]
    total = None
    for base in range(0, state.shape[1], TILE):
        part = dot(state[:, base : base + TILE].astype(BF16), marks_at([index], base, rows))
        total = part if total is None else total + part
    down = total[:, :half]
    up = total[:, half:]
    even = is_even()
    first[...] = jnp.where(even, down, up).astype(BF16)
    second[...] = jnp.where(even, up, down).astype(BF16)


def rims(first, second):
    even = is_even()
    one = first[...].astype(F32)
    two = second[...].astype(F32)
    both = jnp.concatenate([jnp.where(even, one, two), jnp.where(even, two, one)], axis=1)
    return both.astype(BF16)


def fetch(source, target, sem):
    copy = pltpu.make_async_copy(source, target, sem)
    copy.start()
    return copy


def fetch_all(pairs, sems):
    return [fetch(source, target, sems.at[i]) for i, (source, target) in enumerate(pairs)]


def wait_all(copies):
    for copy in copies:
        copy.wait()


def air_pack_kernel(atm_groups, air_ref, send_ref, down, up, air, send, sems):
    @pl.when(lax.axis_index("grp") < atm_groups)
    def _():
        wait_all(fetch_all([(send_ref, send), (air_ref, air)], sems))
        pack_into(air, send, down, up)


def sums_of(pool, nbrs, at, width):
    rows = row_marks(TILE, width)
    picks = [n[:, pl.ds(at, width)] for n in nbrs]
    total = None
    for base in range(0, pool.shape[1], TILE):
        part = dot(pool[:, base : base + TILE], marks_at(picks, base, rows))
        total = part if total is None else total + part
    return total


def rim_marks(nbrs, at, width, own):
    picks = [n[:, pl.ds(at, width)] for n in nbrs]
    return marks_at(picks, own, row_marks(TILE, width))


def fill_ends(counts, ends):
    blocks, lanes = counts.shape
    given = cast_row(counts[...])
    upto = jnp.where(
        row_iota(lanes, lanes) <= lax.broadcasted_iota(I32, (lanes, lanes), 1), 1.0, 0.0
    ).astype(BF16)
    within = dot(given, upto)
    whole = dot(given, jnp.ones((lanes, lanes), BF16))
    before = jnp.zeros((1, lanes), F32)
    for j in range(blocks):
        ends[j : j + 1, :] = (within[j : j + 1] + before).astype(I32)
        before = before + whole[j : j + 1]


def interval(order, begin, end):
    return jnp.where((order >= begin) & (order < end), jnp.ones((), BF16), jnp.zeros((), BF16))


def fill_limits(counts, ends, begins_at, ends_at):
    blocks, lanes = counts.shape
    end = jnp.transpose(ends[...].astype(F32)).astype(I32)
    begin = jnp.transpose((ends[...] - counts[...]).astype(F32)).astype(I32)
    for j in range(blocks):
        at = slice(j * lanes, (j + 1) * lanes)
        ends_at[at, :] = jnp.broadcast_to(end[:, j : j + 1], (lanes, lanes)).astype(I16)
        begins_at[at, :] = jnp.broadcast_to(begin[:, j : j + 1], (lanes, lanes)).astype(I16)


def spread_rows(values, begins_at, ends_at, tile):
    columns, lanes = ends_at.shape
    reach = (columns // 2) // TILE
    lane = lax.broadcasted_iota(I32, (TILE, lanes), 1)
    total = None
    for t in range(max(0, tile - reach), min(tile, columns // TILE - 1) + 1):
        at = slice(t * TILE, (t + 1) * TILE)
        sides = []
        for side in range(TILE // lanes):
            order = (lane + (tile * TILE + side * lanes)).astype(I16)
            sides.append(interval(order, begins_at[at, :], ends_at[at, :]))
        part = dot(values[:, at], jnp.concatenate(sides, axis=1))
        total = part if total is None else total + part
    return total


def gather_rows(values, counts, ends, tile):
    blocks, lanes = counts.shape
    reach = (blocks * lanes // 2) // TILE
    each = TILE // lanes
    end = jnp.concatenate([ends[tile * each + i : tile * each + i + 1, :] for i in range(each)], axis=1)
    count = jnp.concatenate(
        [counts[tile * each + i : tile * each + i + 1, :] for i in range(each)], axis=1
    )
    begin = (end - count).astype(I16)
    end = end.astype(I16)
    rows = row_iota(TILE, TILE)
    total = None
    for t in range(tile, tile + reach + 1):
        mark = interval((rows + t * TILE).astype(I16), begin, end)
        part = dot(values[:, t * TILE : (t + 1) * TILE], mark)
        total = part if total is None else total + part
    return total


def slots_of(owner, seen, visit):
    for o in range(seen.shape[0]):
        seen[o] = 0
    for b in range(owner.shape[1]):
        o = owner[0, b]
        k = seen[o]
        seen[o] = k + 1
        visit(b, o, k)


def look_up(sea, ret_weight, recv, returned, looked):
    cells = sea.shape[1]
    fields = ret_weight.shape[0]
    his = cells // TILE
    pad = returned.shape[0] // his
    for h in range(his):
        chunk = exact(ret_weight[...], sea[:, h * TILE : (h + 1) * TILE])
        chunk = jnp.concatenate([chunk, jnp.zeros((pad - fields, TILE), F32)], axis=0)
        returned[h * pad : (h + 1) * pad, :] = chunk.astype(BF16)
    senders, slots, block = recv.shape
    for s in range(senders):
        index = jnp.concatenate([recv[s, k : k + 1, :] for k in range(slots)], axis=1)
        top = index // TILE
        rest = cast_row(index - top * TILE)
        found = dot(returned[...], one_hot(row_marks(TILE, slots * block), rest))
        look = jnp.zeros((pad, slots * block), F32)
        for h in range(his):
            look = jnp.where(top == h, found[h * pad : (h + 1) * pad], look)
        look = jnp.concatenate(
            [look, jnp.zeros((looked.shape[2] - pad, slots * block), F32)], axis=0
        ).astype(BF16)
        for k in range(slots):
            looked[s, k] = look[:, k * block : (k + 1) * block]


def air_own_kernel(
    atm_groups, after, air_ref, air_nbrs_ref, air_mix_ref, part, marks, air, air_nbrs, air_mix, pool, sems
):
    @pl.when(lax.axis_index("grp") < atm_groups)
    def _():
        near, *rest = fetch_all(
            [(air_nbrs_ref, air_nbrs), (air_ref, air), (air_mix_ref, air_mix)], sems
        )
        amount, columns = air_nbrs.shape
        nbrs = [air_nbrs.at[k : k + 1, :] for k in range(amount)]
        near.wait()
        for at in range(0, columns, TILE):
            marks[:, at : at + TILE] = rim_marks(nbrs, at, TILE, columns)
        wait_all(rest)
        pool[...] = air[...].astype(BF16)
        for at in range(0, columns, TILE):
            total = sums_of(pool, nbrs, at, TILE)
            own = air[:, at : at + TILE]
            mix = air_mix[:, at : at + TILE]
            part[:, at : at + TILE] = own + mix * (total * (1.0 / amount) - own)


def mid_kernel(
    atm_groups, amount,
    first, second, part, marks, air_ref, air_mix_ref, counts_ref, flux_weight_ref, weights_ref, owner,
    sea_ref, sea_send_ref, ret_weight_ref, recv_ref,
    payload, air_out, sea_down_ref, sea_up_ref,
    air, air_mix, counts, flux_weight, weights,
    ends, begins_at, ends_at, values, sent, seen,
    sea, sea_send, ret_weight, recv, returned, down, up, sems, out_sems,
):
    here = lax.axis_index("grp") < atm_groups
    count_groups = sent.shape[0]

    @pl.when(here)
    def _():
        many, *rest = fetch_all(
            [
                (counts_ref, counts),
                (air_mix_ref, air_mix),
                (flux_weight_ref, flux_weight),
                (weights_ref, weights),
            ],
            sems,
        )
        sent[...] = jnp.zeros(sent.shape, BF16)
        values[...] = jnp.zeros(values.shape, BF16)
        rim = rims(first, second)
        many.wait()
        fill_ends(counts, ends)
        fill_limits(counts, ends, begins_at, ends_at)
        wait_all(rest)
        columns = air.shape[1]
        fields = flux_weight.shape[0]
        for at in range(0, columns, TILE):
            total = dot(rim, marks[:, at : at + TILE])
            new = part[:, at : at + TILE] + air_mix[:, at : at + TILE] * (total * (1.0 / amount))
            air[:, at : at + TILE] = new
            hi, lo = split(exact(flux_weight[...], new))
            values[0:fields, at : at + TILE] = hi
            values[32 : 32 + fields, at : at + TILE] = lo
        stored = fetch(air, air_out, out_sems.at[0])
        block = sent.shape[3]
        each = TILE // block
        tiles = []
        for t in range(weights.shape[1] // TILE):
            both = spread_rows(values, begins_at, ends_at, t)
            tile = (both[0:fields] + both[32 : 32 + fields]) * weights[:, t * TILE : (t + 1) * TILE]
            tiles.append(tile.astype(BF16))

        def visit(b, o, k):
            i = b % each
            sent[o, k] = tiles[b // each][:, i * block : (i + 1) * block]

        slots_of(owner, seen, visit)
        done = fetch(sent, payload.at[pl.ds(atm_groups, count_groups)], out_sems.at[1])
        wait_all([stored, done])

    @pl.when(jnp.logical_not(here))
    def _():
        listed, kept, *rest = fetch_all(
            [
                (sea_send_ref, sea_send),
                (air_ref, air),
                (sea_ref, sea),
                (ret_weight_ref, ret_weight),
                (recv_ref, recv),
            ],
            sems,
        )
        wait_all(rest)
        look_up(sea, ret_weight, recv, returned, sent)
        done = fetch(sent, payload.at[pl.ds(0, atm_groups)], out_sems.at[1])
        kept.wait()
        keep = fetch(air, air_out, out_sems.at[0])
        listed.wait()
        pack_into(sea, sea_send, down, up)
        out_down = fetch(down, sea_down_ref, out_sems.at[2])
        out_up = fetch(up, sea_up_ref, out_sems.at[3])
        wait_all([done, keep, out_down, out_up])


def sea_own_kernel(
    atm_groups,
    after, sea_ref, sea_nbrs_ref,
    sums_ref, marks_ref, sea_out,
    sea, sea_nbrs, sums, marks, pool, sems, out_sems,
):
    here = lax.axis_index("grp") < atm_groups

    @pl.when(here)
    def _():
        fetch(sea_ref, sea, sems.at[0]).wait()
        fetch(sea, sea_out, out_sems.at[0]).wait()

    @pl.when(jnp.logical_not(here))
    def _():
        near, whole = fetch_all([(sea_nbrs_ref, sea_nbrs), (sea_ref, sea)], sems)
        amount, _, cells = sea_nbrs.shape
        nbrs = [sea_nbrs.at[k] for k in range(amount)]
        near.wait()
        for at in range(0, cells, TILE):
            marks[:, at : at + TILE] = rim_marks(nbrs, at, TILE, cells)
        out_marks = fetch(marks, marks_ref, out_sems.at[1])
        whole.wait()
        pool[...] = sea[...].astype(BF16)

        def step(i, carry):
            at = pl.multiple_of(i * TILE, TILE)
            sums[:, pl.ds(at, TILE)] = sums_of(pool, nbrs, at, TILE)
            return carry

        lax.fori_loop(0, cells // TILE, step, 0)
        out_sums = fetch(sums, sums_ref, out_sems.at[0])
        wait_all([out_marks, out_sums])


def last_kernel(
    atm_groups, amount,
    arrived, counts_ref, weights_ref, owner,
    recv_ref, sea_ref, sums_ref, marks_ref, first, second, sea_mix_ref, force_weight_ref, sea_in,
    sea_out, mapped_ref,
    counts, ends, weights, mine, mapped, seen,
    recv, sea, sums, marks, sea_mix, force_weight, sems, out_sems,
):
    here = lax.axis_index("grp") < atm_groups
    fields, _, columns = mapped.shape

    @pl.when(here)
    def _():
        many, given = fetch_all([(counts_ref, counts), (weights_ref, weights)], sems)
        block = arrived.shape[3]

        def visit(b, o, k):
            mine[:, b * block : (b + 1) * block] = arrived[atm_groups + o, k].astype(F32)

        slots_of(owner, seen, visit)
        many.wait()
        fill_ends(counts, ends)
        given.wait()
        w = weights[...]
        scaled = mine[0:16, :] * w
        order = row_iota(16, scaled.shape[1])
        scaled = jnp.where(order < fields, scaled, jnp.where(order == fields, w, 0.0))
        hi, lo = split(scaled)
        both_in = jnp.concatenate([hi, lo], axis=0)
        for t in range(columns // TILE):
            both = gather_rows(both_in, counts, ends, t)
            both = both[0:16] + both[16:32]
            mean = both[0:fields] / both[fields : fields + 1]
            for f in range(fields):
                mapped[f, :, t * TILE : (t + 1) * TILE] = mean[f : f + 1]
        fetch(mapped, mapped_ref, out_sems.at[0]).wait()

    @pl.when(jnp.logical_not(here))
    def _():
        mapped[...] = jnp.zeros(mapped.shape, F32)
        stored = fetch(mapped, mapped_ref, out_sems.at[0])
        cells_in, *rest = fetch_all(
            [
                (recv_ref, recv),
                (sea_ref, sea),
                (sums_ref, sums),
                (marks_ref, marks),
                (sea_mix_ref, sea_mix),
                (force_weight_ref, force_weight),
            ],
            sems,
        )
        senders, slots, block = recv.shape
        rows = arrived.shape[2]
        his = sea.shape[1] // TILE
        flux = jnp.zeros((his * rows, TILE), F32)
        cells_in.wait()
        for s in range(senders):
            index = jnp.concatenate([recv[s, k : k + 1, :] for k in range(slots)], axis=1)
            top = index // TILE
            rest_of = cast_row(index - top * TILE)
            values = jnp.concatenate([arrived[s, k].astype(F32) for k in range(slots)], axis=1)
            parts = [jnp.where(top == h, values, 0.0) for h in range(his)]
            apart = jnp.concatenate(parts, axis=0).astype(BF16)
            flux = flux + dot_nt(apart, one_hot(row_marks(TILE, slots * block), rest_of))
        wait_all(rest)
        rim = rims(first, second)
        spread_weight = jnp.transpose(force_weight[...])
        for h in range(his):
            at = slice(h * TILE, (h + 1) * TILE)
            forcing = exact(spread_weight, flux[h * rows : (h + 1) * rows])
            total = sums[:, at] + dot(rim, marks[:, at])
            own = sea[:, at]
            sea[:, at] = own + sea_mix[:, at] * (total * (1.0 / amount) - own) + forcing
        out = fetch(sea, sea_out, out_sems.at[1])
        wait_all([stored, out])


def vmem():
    return pl.BlockSpec(memory_space=pltpu.VMEM)


def smem():
    return pl.BlockSpec(memory_space=pltpu.SMEM)


def anywhere():
    return pl.BlockSpec(memory_space=pl.ANY)


def in_hbm(x):
    return pltpu.with_memory_space_constraint(x, pltpu.HBM)


def shape(dims, dtype):
    return jax.ShapeDtypeStruct(dims, dtype)


def on_device(
    atm_state, atm_nbrs, atm_send, atm_mix, flux_weight, margin_counts, margin_weight,
    block_owner, recv_cols, ocn_state, ocn_nbrs, ocn_send, ocn_mix, force_weight, ret_weight,
):
    levels_air, columns = atm_state.shape[2:]
    levels_sea, cells = ocn_state.shape[2:]
    pair = atm_send.shape[2]
    half = pair // 2
    amount_air = atm_nbrs.shape[2]
    amount_sea = ocn_nbrs.shape[2]
    atm_groups, capacity, block = recv_cols.shape[2:]
    row_count = margin_weight.shape[2]
    blocks_here = block_owner.shape[2]
    fields = flux_weight.shape[0]
    ret_fields = ret_weight.shape[0]
    groups = lax.axis_size("grp")
    peers = lax.axis_size("dev")

    air = in_hbm(atm_state.reshape(levels_air, columns))
    sea = in_hbm(ocn_state.reshape(levels_sea, cells))
    counts = in_hbm(margin_counts.reshape(columns // 128, 128))
    weights = in_hbm(margin_weight.reshape(1, row_count))
    owner = in_hbm(block_owner.reshape(1, blocks_here))
    recv = in_hbm(recv_cols.reshape(atm_groups, capacity, block))
    air_mix = in_hbm(atm_mix.reshape(1, columns))
    air_shape = shape((levels_air, columns), F32)
    sea_shape = shape((levels_sea, cells), F32)
    air_rim = shape((levels_air, half), BF16)
    sea_rim = shape((levels_sea, half), BF16)
    payload_shape = shape((groups, capacity, fields, block), BF16)
    sent_shape = (capacity, fields, block)
    dma = pltpu.SemaphoreType.DMA

    def scratch(*dims, dtype=F32):
        return pltpu.VMEM(dims, dtype)

    air_scratch = scratch(levels_air, columns)
    sea_scratch = scratch(levels_sea, cells)
    sea_marks_in = scratch(pair, cells, dtype=BF16)
    counts_in = scratch(columns // 128, 128, dtype=I32)
    sea_half = scratch(levels_sea, half, dtype=BF16)
    pair_in = scratch(1, pair, dtype=I32)
    recv_in = scratch(atm_groups, capacity, block, dtype=I32)
    weights_in = scratch(1, row_count)
    air_row = scratch(1, columns)
    params = pltpu.CompilerParams(vmem_limit_bytes=24 * 2**20)

    def swapped(value, first, last, odd):
        pairs = [
            (g * peers + i, g * peers + (((i - odd) ^ 1) + odd) % peers)
            for g in range(first, last)
            for i in range(peers)
        ]
        return lax.ppermute(value, ("grp", "dev"), pairs)

    to_first, to_second = pl.pallas_call(
        functools.partial(air_pack_kernel, atm_groups),
        out_shape=[air_rim] * 2,
        in_specs=[anywhere()] * 2,
        out_specs=[vmem(), vmem()],
        scratch_shapes=[air_scratch, pair_in, dma((2,))],
        compiler_params=params,
        name="air_pack",
    )(air, in_hbm(atm_send.reshape(1, pair)))
    first = swapped(to_first, 0, atm_groups, 1)
    second = swapped(to_second, 0, atm_groups, 0)

    part, marks = pl.pallas_call(
        functools.partial(air_own_kernel, atm_groups),
        out_shape=[air_shape, shape((pair, columns), BF16)],
        in_specs=[anywhere()] * 4,
        out_specs=[vmem()] * 2,
        scratch_shapes=[
            air_scratch,
            scratch(amount_air, columns, dtype=I32),
            air_row,
            scratch(levels_air, columns, dtype=BF16),
            dma((3,)),
        ],
        compiler_params=params,
        cost_estimate=pl.CostEstimate(flops=4 * 10**9, bytes_accessed=10**7, transcendentals=0),
        name="air_own",
    )(to_second, air, in_hbm(atm_nbrs.reshape(amount_air, columns)), air_mix)
    payload, air_next, sea_to_first, sea_to_second = pl.pallas_call(
        functools.partial(mid_kernel, atm_groups, amount_air),
        out_shape=[payload_shape, air_shape, sea_rim, sea_rim],
        in_specs=[vmem()] * 4 + [anywhere()] * 5 + [smem()] + [anywhere()] * 4,
        out_specs=[anywhere()] * 4,
        scratch_shapes=[
            air_scratch,
            air_row,
            counts_in,
            scratch(fields, levels_air),
            weights_in,
            counts_in,
            scratch(columns, 128, dtype=I16),
            scratch(columns, 128, dtype=I16),
            scratch(64, columns, dtype=BF16),
            scratch(atm_groups, *sent_shape, dtype=BF16),
            pltpu.SMEM((groups - atm_groups,), I32),
            sea_scratch,
            pair_in,
            scratch(ret_fields, levels_sea),
            recv_in,
            scratch(16 * (cells // TILE), TILE, dtype=BF16),
            sea_half,
            sea_half,
            dma((5,)),
            dma((4,)),
        ],
        compiler_params=params,
        name="mid",
    )(
        first, second, part, marks, air, air_mix, counts, in_hbm(flux_weight),
        weights, owner, sea, in_hbm(ocn_send.reshape(1, pair)), in_hbm(ret_weight), recv,
    )
    arrived = lax.all_to_all(payload, "grp", split_axis=0, concat_axis=0, tiled=True)
    sea_first = swapped(sea_to_first, atm_groups, groups, 1)
    sea_second = swapped(sea_to_second, atm_groups, groups, 0)

    sums, sea_marks, sea_pre = pl.pallas_call(
        functools.partial(sea_own_kernel, atm_groups),
        out_shape=[sea_shape, shape((pair, cells), BF16), sea_shape],
        in_specs=[anywhere()] * 3,
        out_specs=[anywhere()] * 3,
        scratch_shapes=[
            sea_scratch,
            scratch(amount_sea, 1, cells, dtype=I32),
            sea_scratch,
            sea_marks_in,
            scratch(levels_sea, cells, dtype=BF16),
            dma((2,)),
            dma((2,)),
        ],
        compiler_params=params,
        cost_estimate=pl.CostEstimate(flops=8 * 10**9, bytes_accessed=10**7, transcendentals=0),
        name="sea_own",
    )(payload, sea, in_hbm(ocn_nbrs.reshape(amount_sea, 1, cells)))
    sea_next, mapped = pl.pallas_call(
        functools.partial(last_kernel, atm_groups, amount_sea),
        out_shape=[sea_shape, shape((ret_fields, 1, columns), F32)],
        in_specs=[vmem()] + [anywhere()] * 2 + [smem()] + [anywhere()] * 4 + [vmem()] * 2 + [anywhere()] * 3,
        out_specs=[anywhere()] * 2,
        scratch_shapes=[
            counts_in,
            counts_in,
            weights_in,
            scratch(fields, row_count),
            scratch(ret_fields, 1, columns),
            pltpu.SMEM((groups - atm_groups,), I32),
            recv_in,
            sea_scratch,
            sea_scratch,
            sea_marks_in,
            scratch(1, cells),
            scratch(fields, levels_sea),
            dma((6,)),
            dma((2,)),
        ],
        input_output_aliases={12: 0},
        compiler_params=params,
        name="last",
    )(
        arrived, counts, weights, owner,
        recv, sea, sums, sea_marks, sea_first, sea_second, in_hbm(ocn_mix.reshape(1, cells)), in_hbm(force_weight.T),
        sea_pre,
    )
    mapped = mapped.reshape(1, 1, ret_fields, columns)
    return (air_next[None, None], sea_next[None, None], mapped)


def solution(mesh):
    whole = P("grp", "dev")
    specs = [whole] * 15
    for replicated in (4, 13, 14):
        specs[replicated] = P()
    return jax.shard_map(
        on_device,
        mesh=mesh,
        in_specs=tuple(specs),
        out_specs=(whole, whole, whole),
        check_vma=False,
    )
```

```python
import functools

import jax
import jax.numpy as jnp
from jax import lax
from jax.experimental import pallas as pl
from jax.experimental.pallas import tpu as pltpu
from jax.sharding import PartitionSpec as P

F32 = jnp.float32
BF16 = jnp.bfloat16
I32 = jnp.int32
I16 = jnp.int16
TILE = 256
NT = (((1,), (1,)), ((), ()))


def dot(a, b):
    return jnp.dot(a, b, preferred_element_type=F32)


def dot_nt(a, b):
    return lax.dot_general(a, b, NT, preferred_element_type=F32)


def split(x):
    hi = x.astype(BF16)
    lo = (x - hi.astype(F32)).astype(BF16)
    return hi, lo


def exact(w, x):
    wh, wl = split(w)
    xh, xl = split(x)
    return dot(wh, xh) + (dot(wl, xh) + dot(wh, xl))


def row_iota(rows, cols):
    return lax.broadcasted_iota(I32, (rows, cols), 0)


def one_hot(rows_bf, index_row):
    return jnp.where(rows_bf == index_row, jnp.ones((), BF16), jnp.zeros((), BF16))


def cast_row(row):
    return row.astype(F32).astype(BF16)


def row_marks(rows, cols):
    return cast_row(row_iota(rows, cols))


def marks_at(picks, base, rows):
    marks = None
    for pick in picks:
        mark = one_hot(rows, cast_row(pick - base))
        marks = mark if marks is None else marks + mark
    return marks


def is_even():
    return lax.rem(lax.axis_index("dev"), 2) == 0


def pack_into(state, send, first, second):
    half = first.shape[1]
    rows = row_marks(TILE, 2 * half)
    index = send[...]
    total = None
    for base in range(0, state.shape[1], TILE):
        part = dot(state[:, base : base + TILE].astype(BF16), marks_at([index], base, rows))
        total = part if total is None else total + part
    down = total[:, :half]
    up = total[:, half:]
    even = is_even()
    first[...] = jnp.where(even, down, up).astype(BF16)
    second[...] = jnp.where(even, up, down).astype(BF16)


def rims(first, second):
    even = is_even()
    one = first[...].astype(F32)
    two = second[...].astype(F32)
    both = jnp.concatenate([jnp.where(even, one, two), jnp.where(even, two, one)], axis=1)
    return both.astype(BF16)


def fetch(source, target, sem):
    copy = pltpu.make_async_copy(source, target, sem)
    copy.start()
    return copy


def fetch_all(pairs, sems):
    return [fetch(source, target, sems.at[i]) for i, (source, target) in enumerate(pairs)]


def wait_all(copies):
    for copy in copies:
        copy.wait()


def air_pack_kernel(atm_groups, air_ref, send_ref, down, up, air, send, sems):
    @pl.when(lax.axis_index("grp") < atm_groups)
    def _():
        wait_all(fetch_all([(send_ref, send), (air_ref, air)], sems))
        pack_into(air, send, down, up)


def sums_of(pool, nbrs, at, width):
    rows = row_marks(TILE, width)
    picks = [n[:, pl.ds(at, width)] for n in nbrs]
    total = None
    for base in range(0, pool.shape[1], TILE):
        part = dot(pool[:, base : base + TILE], marks_at(picks, base, rows))
        total = part if total is None else total + part
    return total


def rim_marks(nbrs, at, width, own):
    picks = [n[:, pl.ds(at, width)] for n in nbrs]
    return marks_at(picks, own, row_marks(TILE, width))


def fill_ends(counts, ends):
    blocks, lanes = counts.shape
    given = cast_row(counts[...])
    upto = jnp.where(
        row_iota(lanes, lanes) <= lax.broadcasted_iota(I32, (lanes, lanes), 1), 1.0, 0.0
    ).astype(BF16)
    within = dot(given, upto)
    whole = dot(given, jnp.ones((lanes, lanes), BF16))
    before = jnp.zeros((1, lanes), F32)
    for j in range(blocks):
        ends[j : j + 1, :] = (within[j : j + 1] + before).astype(I32)
        before = before + whole[j : j + 1]


def interval(order, begin, end):
    return jnp.where((order >= begin) & (order < end), jnp.ones((), BF16), jnp.zeros((), BF16))


def fill_limits(counts, ends, begins_at, ends_at):
    blocks, lanes = counts.shape
    end = jnp.transpose(ends[...].astype(F32)).astype(I32)
    begin = jnp.transpose((ends[...] - counts[...]).astype(F32)).astype(I32)
    for j in range(blocks):
        at = slice(j * lanes, (j + 1) * lanes)
        ends_at[at, :] = jnp.broadcast_to(end[:, j : j + 1], (lanes, lanes)).astype(I16)
        begins_at[at, :] = jnp.broadcast_to(begin[:, j : j + 1], (lanes, lanes)).astype(I16)


def spans(columns):
    reach = (columns // 2) // TILE
    amount = columns // TILE
    return [
        (p, list(range(max(0, p - reach), min(p, amount - 1) + 1))) for p in range(amount + reach)
    ]


def fill_spread(begins_at, ends_at, tiles):
    columns, lanes = ends_at.shape
    lane = lax.broadcasted_iota(I32, (TILE, lanes), 1)
    i = 0
    for p, near in spans(columns):
        for t in near:
            at = slice(t * TILE, (t + 1) * TILE)
            for side in range(0, TILE, lanes):
                order = (lane + (p * TILE + side)).astype(I16)
                tiles[i * TILE : (i + 1) * TILE, side : side + lanes] = interval(
                    order, begins_at[at, :], ends_at[at, :]
                )
            i += 1


def fill_gather(counts, ends, tiles):
    blocks, lanes = counts.shape
    each = TILE // lanes
    limits = []
    for t in range(blocks // each):
        lines = range(t * each, (t + 1) * each)
        end = jnp.concatenate([ends[i : i + 1, :] for i in lines], axis=1)
        count = jnp.concatenate([counts[i : i + 1, :] for i in lines], axis=1)
        limits.append(((end - count).astype(I16), end.astype(I16)))
    rows = row_iota(TILE, TILE)
    i = 0
    for p, near in spans(blocks * lanes):
        order = (rows + p * TILE).astype(I16)
        for t in near:
            tiles[i * TILE : (i + 1) * TILE, :] = interval(order, *limits[t])
            i += 1


def slots_of(owner, seen, visit):
    for o in range(seen.shape[0]):
        seen[o] = 0
    for b in range(owner.shape[1]):
        o = owner[0, b]
        k = seen[o]
        seen[o] = k + 1
        visit(b, o, k)


def look_up(sea, ret_weight, recv, returned, looked):
    cells = sea.shape[1]
    fields = ret_weight.shape[0]
    his = cells // TILE
    pad = returned.shape[0] // his
    for h in range(his):
        chunk = exact(ret_weight[...], sea[:, h * TILE : (h + 1) * TILE])
        chunk = jnp.concatenate([chunk, jnp.zeros((pad - fields, TILE), F32)], axis=0)
        returned[h * pad : (h + 1) * pad, :] = chunk.astype(BF16)
    senders, slots, block = recv.shape
    for s in range(senders):
        index = jnp.concatenate([recv[s, k : k + 1, :] for k in range(slots)], axis=1)
        top = index // TILE
        rest = cast_row(index - top * TILE)
        found = dot(returned[...], one_hot(row_marks(TILE, slots * block), rest))
        look = jnp.zeros((pad, slots * block), F32)
        for h in range(his):
            look = jnp.where(top == h, found[h * pad : (h + 1) * pad], look)
        look = jnp.concatenate(
            [look, jnp.zeros((looked.shape[2] - pad, slots * block), F32)], axis=0
        ).astype(BF16)
        for k in range(slots):
            looked[s, k] = look[:, k * block : (k + 1) * block]


def air_own_kernel(
    atm_groups,
    after, air_ref, air_nbrs_ref, air_mix_ref, counts_ref, flux_weight_ref, weights_ref,
    part, marks, tiles, air_mix, flux_weight, weights,
    air, air_nbrs, counts, ends, begins_at, ends_at, pool, sems,
):
    @pl.when(lax.axis_index("grp") < atm_groups)
    def _():
        many, near, whole, mixed, *rest = fetch_all(
            [
                (counts_ref, counts),
                (air_nbrs_ref, air_nbrs),
                (air_ref, air),
                (air_mix_ref, air_mix),
                (flux_weight_ref, flux_weight),
                (weights_ref, weights),
            ],
            sems,
        )
        amount, columns = air_nbrs.shape
        nbrs = [air_nbrs.at[k : k + 1, :] for k in range(amount)]
        many.wait()
        fill_ends(counts, ends)
        fill_limits(counts, ends, begins_at, ends_at)
        fill_spread(begins_at, ends_at, tiles)
        near.wait()
        for at in range(0, columns, TILE):
            marks[:, at : at + TILE] = rim_marks(nbrs, at, TILE, columns)
        wait_all([whole, mixed])
        pool[...] = air[...].astype(BF16)
        for at in range(0, columns, TILE):
            total = sums_of(pool, nbrs, at, TILE)
            own = air[:, at : at + TILE]
            mix = air_mix[:, at : at + TILE]
            part[:, at : at + TILE] = own + mix * (total * (1.0 / amount) - own)
        wait_all(rest)


def mid_kernel(
    atm_groups, amount,
    first, second, part, marks, tiles, air_mix, flux_weight, weights, air_ref, owner_ref,
    sea_ref, sea_send_ref, ret_weight_ref, recv_ref,
    payload, air_out, sea_down_ref, sea_up_ref,
    air, values, sent, owner, seen,
    sea, sea_send, ret_weight, recv, returned, down, up, sems, out_sems,
):
    here = lax.axis_index("grp") < atm_groups
    count_groups = sent.shape[0]

    @pl.when(here)
    def _():
        owned = fetch(owner_ref, owner, sems.at[0])
        sent[...] = jnp.zeros(sent.shape, BF16)
        values[...] = jnp.zeros(values.shape, BF16)
        rim = rims(first, second)
        columns = air.shape[1]
        fields = flux_weight.shape[0]
        for at in range(0, columns, TILE):
            total = dot(rim, marks[:, at : at + TILE])
            new = part[:, at : at + TILE] + air_mix[:, at : at + TILE] * (total * (1.0 / amount))
            air[:, at : at + TILE] = new
            hi, lo = split(exact(flux_weight[...], new))
            values[0:fields, at : at + TILE] = hi
            values[32 : 32 + fields, at : at + TILE] = lo
        stored = fetch(air, air_out, out_sems.at[0])
        block = sent.shape[3]
        each = TILE // block
        made = []
        i = 0
        for p, near in spans(columns):
            both = None
            for t in near:
                one = values[:, t * TILE : (t + 1) * TILE]
                more = dot(one, tiles[i * TILE : (i + 1) * TILE, :])
                both = more if both is None else both + more
                i += 1
            tile = (both[0:fields] + both[32 : 32 + fields]) * weights[:, p * TILE : (p + 1) * TILE]
            made.append(tile.astype(BF16))

        def visit(b, o, k):
            i = b % each
            sent[o, k] = made[b // each][:, i * block : (i + 1) * block]

        owned.wait()
        slots_of(owner, seen, visit)
        done = fetch(sent, payload.at[pl.ds(atm_groups, count_groups)], out_sems.at[1])
        wait_all([stored, done])

    @pl.when(jnp.logical_not(here))
    def _():
        listed, kept, *rest = fetch_all(
            [
                (sea_send_ref, sea_send),
                (air_ref, air),
                (sea_ref, sea),
                (ret_weight_ref, ret_weight),
                (recv_ref, recv),
            ],
            sems,
        )
        wait_all(rest)
        look_up(sea, ret_weight, recv, returned, sent)
        done = fetch(sent, payload.at[pl.ds(0, atm_groups)], out_sems.at[1])
        kept.wait()
        keep = fetch(air, air_out, out_sems.at[0])
        listed.wait()
        pack_into(sea, sea_send, down, up)
        out_down = fetch(down, sea_down_ref, out_sems.at[2])
        out_up = fetch(up, sea_up_ref, out_sems.at[3])
        wait_all([done, keep, out_down, out_up])


def sea_own_kernel(
    atm_groups,
    after, sea_ref, sea_nbrs_ref, counts_ref, weights_ref,
    sums_ref, marks_ref, sea_out, tiles, weights,
    sea, sea_nbrs, sums, marks, pool, counts, ends, sems, out_sems,
):
    here = lax.axis_index("grp") < atm_groups

    @pl.when(here)
    def _():
        whole, many, given = fetch_all(
            [(sea_ref, sea), (counts_ref, counts), (weights_ref, weights)], sems
        )
        whole.wait()
        keep = fetch(sea, sea_out, out_sems.at[0])
        many.wait()
        fill_ends(counts, ends)
        fill_gather(counts, ends, tiles)
        wait_all([given, keep])

    @pl.when(jnp.logical_not(here))
    def _():
        near, whole = fetch_all([(sea_nbrs_ref, sea_nbrs), (sea_ref, sea)], sems)
        amount, _, cells = sea_nbrs.shape
        nbrs = [sea_nbrs.at[k] for k in range(amount)]
        near.wait()
        for at in range(0, cells, TILE):
            marks[:, at : at + TILE] = rim_marks(nbrs, at, TILE, cells)
        out_marks = fetch(marks, marks_ref, out_sems.at[1])
        whole.wait()
        pool[...] = sea[...].astype(BF16)

        def step(i, carry):
            at = pl.multiple_of(i * TILE, TILE)
            sums[:, pl.ds(at, TILE)] = sums_of(pool, nbrs, at, TILE)
            return carry

        lax.fori_loop(0, cells // TILE, step, 0)
        out_sums = fetch(sums, sums_ref, out_sems.at[0])
        wait_all([out_marks, out_sums])


def last_kernel(
    atm_groups, amount,
    arrived, tiles, weights, owner_ref,
    recv_ref, sea_ref, sums_ref, marks_ref, first, second, sea_mix_ref, force_weight_ref, sea_in,
    sea_out, mapped_ref,
    mine, mapped, owner, seen,
    recv, sea, sums, marks, sea_mix, force_weight, sems, out_sems,
):
    here = lax.axis_index("grp") < atm_groups
    fields, _, columns = mapped.shape

    @pl.when(here)
    def _():
        owned = fetch(owner_ref, owner, sems.at[0])
        block = arrived.shape[3]

        def visit(b, o, k):
            mine[:, b * block : (b + 1) * block] = arrived[atm_groups + o, k].astype(F32)

        owned.wait()
        slots_of(owner, seen, visit)
        w = weights[...]
        scaled = mine[0:16, :] * w
        order = row_iota(16, scaled.shape[1])
        scaled = jnp.where(order < fields, scaled, jnp.where(order == fields, w, 0.0))
        hi, lo = split(scaled)
        both_in = jnp.concatenate([hi, lo], axis=0)
        sums_in = [None] * (columns // TILE)
        i = 0
        for p, near in spans(columns):
            for t in near:
                more = dot(both_in[:, p * TILE : (p + 1) * TILE], tiles[i * TILE : (i + 1) * TILE, :])
                sums_in[t] = more if sums_in[t] is None else sums_in[t] + more
                i += 1
        for t, both in enumerate(sums_in):
            both = both[0:16] + both[16:32]
            mean = both[0:fields] / both[fields : fields + 1]
            for f in range(fields):
                mapped[f, :, t * TILE : (t + 1) * TILE] = mean[f : f + 1]
        fetch(mapped, mapped_ref, out_sems.at[0]).wait()

    @pl.when(jnp.logical_not(here))
    def _():
        mapped[...] = jnp.zeros(mapped.shape, F32)
        stored = fetch(mapped, mapped_ref, out_sems.at[0])
        cells_in, *rest = fetch_all(
            [
                (recv_ref, recv),
                (sea_ref, sea),
                (sums_ref, sums),
                (marks_ref, marks),
                (sea_mix_ref, sea_mix),
                (force_weight_ref, force_weight),
            ],
            sems,
        )
        senders, slots, block = recv.shape
        rows = arrived.shape[2]
        his = sea.shape[1] // TILE
        flux = jnp.zeros((his * rows, TILE), F32)
        cells_in.wait()
        for s in range(senders):
            index = jnp.concatenate([recv[s, k : k + 1, :] for k in range(slots)], axis=1)
            top = index // TILE
            rest_of = cast_row(index - top * TILE)
            values = jnp.concatenate([arrived[s, k].astype(F32) for k in range(slots)], axis=1)
            parts = [jnp.where(top == h, values, 0.0) for h in range(his)]
            apart = jnp.concatenate(parts, axis=0).astype(BF16)
            flux = flux + dot_nt(apart, one_hot(row_marks(TILE, slots * block), rest_of))
        wait_all(rest)
        rim = rims(first, second)
        spread_weight = jnp.transpose(force_weight[...])
        for h in range(his):
            at = slice(h * TILE, (h + 1) * TILE)
            forcing = exact(spread_weight, flux[h * rows : (h + 1) * rows])
            total = sums[:, at] + dot(rim, marks[:, at])
            own = sea[:, at]
            sea[:, at] = own + sea_mix[:, at] * (total * (1.0 / amount) - own) + forcing
        out = fetch(sea, sea_out, out_sems.at[1])
        wait_all([stored, out])


def vmem():
    return pl.BlockSpec(memory_space=pltpu.VMEM)


def anywhere():
    return pl.BlockSpec(memory_space=pl.ANY)


def in_hbm(x):
    return pltpu.with_memory_space_constraint(x, pltpu.HBM)


def shape(dims, dtype):
    return jax.ShapeDtypeStruct(dims, dtype)


def on_device(
    atm_state, atm_nbrs, atm_send, atm_mix, flux_weight, margin_counts, margin_weight,
    block_owner, recv_cols, ocn_state, ocn_nbrs, ocn_send, ocn_mix, force_weight, ret_weight,
):
    levels_air, columns = atm_state.shape[2:]
    levels_sea, cells = ocn_state.shape[2:]
    pair = atm_send.shape[2]
    half = pair // 2
    amount_air = atm_nbrs.shape[2]
    amount_sea = ocn_nbrs.shape[2]
    atm_groups, capacity, block = recv_cols.shape[2:]
    row_count = margin_weight.shape[2]
    blocks_here = block_owner.shape[2]
    fields = flux_weight.shape[0]
    ret_fields = ret_weight.shape[0]
    groups = lax.axis_size("grp")
    peers = lax.axis_size("dev")

    air = in_hbm(atm_state.reshape(levels_air, columns))
    sea = in_hbm(ocn_state.reshape(levels_sea, cells))
    counts = in_hbm(margin_counts.reshape(columns // 128, 128))
    weights = in_hbm(margin_weight.reshape(1, row_count))
    owner = in_hbm(block_owner.reshape(1, blocks_here))
    recv = in_hbm(recv_cols.reshape(atm_groups, capacity, block))
    air_mix = in_hbm(atm_mix.reshape(1, columns))
    air_shape = shape((levels_air, columns), F32)
    sea_shape = shape((levels_sea, cells), F32)
    air_rim = shape((levels_air, half), BF16)
    sea_rim = shape((levels_sea, half), BF16)
    payload_shape = shape((groups, capacity, fields, block), BF16)
    sent_shape = (capacity, fields, block)
    dma = pltpu.SemaphoreType.DMA
    tile_count = sum(len(near) for _, near in spans(columns))
    tiles_shape = shape((tile_count * TILE, TILE), BF16)
    owner_in = pltpu.SMEM((1, blocks_here), I32)

    def scratch(*dims, dtype=F32):
        return pltpu.VMEM(dims, dtype)

    air_scratch = scratch(levels_air, columns)
    sea_scratch = scratch(levels_sea, cells)
    sea_marks_in = scratch(pair, cells, dtype=BF16)
    counts_in = scratch(columns // 128, 128, dtype=I32)
    sea_half = scratch(levels_sea, half, dtype=BF16)
    pair_in = scratch(1, pair, dtype=I32)
    recv_in = scratch(atm_groups, capacity, block, dtype=I32)
    params = pltpu.CompilerParams(vmem_limit_bytes=24 * 2**20)

    def swapped(value, first, last, odd):
        pairs = [
            (g * peers + i, g * peers + (((i - odd) ^ 1) + odd) % peers)
            for g in range(first, last)
            for i in range(peers)
        ]
        return lax.ppermute(value, ("grp", "dev"), pairs)

    to_first, to_second = pl.pallas_call(
        functools.partial(air_pack_kernel, atm_groups),
        out_shape=[air_rim] * 2,
        in_specs=[anywhere()] * 2,
        out_specs=[vmem(), vmem()],
        scratch_shapes=[air_scratch, pair_in, dma((2,))],
        compiler_params=params,
        name="air_pack",
    )(air, in_hbm(atm_send.reshape(1, pair)))
    first = swapped(to_first, 0, atm_groups, 1)
    second = swapped(to_second, 0, atm_groups, 0)

    part, marks, tiles, mix, flux_in, weights_here = pl.pallas_call(
        functools.partial(air_own_kernel, atm_groups),
        out_shape=[
            air_shape,
            shape((pair, columns), BF16),
            tiles_shape,
            shape((1, columns), F32),
            shape((fields, levels_air), F32),
            shape((1, row_count), F32),
        ],
        in_specs=[anywhere()] * 7,
        out_specs=[vmem()] * 6,
        scratch_shapes=[
            air_scratch,
            scratch(amount_air, columns, dtype=I32),
            counts_in,
            counts_in,
            scratch(columns, 128, dtype=I16),
            scratch(columns, 128, dtype=I16),
            scratch(levels_air, columns, dtype=BF16),
            dma((6,)),
        ],
        compiler_params=params,
        cost_estimate=pl.CostEstimate(flops=4 * 10**9, bytes_accessed=10**7, transcendentals=0),
        name="air_own",
    )(
        to_second, air, in_hbm(atm_nbrs.reshape(amount_air, columns)), air_mix, counts,
        in_hbm(flux_weight), weights,
    )
    payload, air_next, sea_to_first, sea_to_second = pl.pallas_call(
        functools.partial(mid_kernel, atm_groups, amount_air),
        out_shape=[payload_shape, air_shape, sea_rim, sea_rim],
        in_specs=[vmem()] * 8 + [anywhere()] * 6,
        out_specs=[anywhere()] * 4,
        scratch_shapes=[
            air_scratch,
            scratch(64, columns, dtype=BF16),
            scratch(atm_groups, *sent_shape, dtype=BF16),
            owner_in,
            pltpu.SMEM((groups - atm_groups,), I32),
            sea_scratch,
            pair_in,
            scratch(ret_fields, levels_sea),
            recv_in,
            scratch(16 * (cells // TILE), TILE, dtype=BF16),
            sea_half,
            sea_half,
            dma((5,)),
            dma((4,)),
        ],
        compiler_params=params,
        name="mid",
    )(
        first, second, part, marks, tiles, mix, flux_in, weights_here, air, owner, sea, in_hbm(ocn_send.reshape(1, pair)), in_hbm(ret_weight), recv,
    )
    arrived = lax.all_to_all(payload, "grp", split_axis=0, concat_axis=0, tiled=True)
    sea_first = swapped(sea_to_first, atm_groups, groups, 1)
    sea_second = swapped(sea_to_second, atm_groups, groups, 0)

    sums, sea_marks, sea_pre, back_tiles, weights_back = pl.pallas_call(
        functools.partial(sea_own_kernel, atm_groups),
        out_shape=[
            sea_shape,
            shape((pair, cells), BF16),
            sea_shape,
            tiles_shape,
            shape((1, row_count), F32),
        ],
        in_specs=[anywhere()] * 5,
        out_specs=[pl.BlockSpec(memory_space=pltpu.HBM)] + [anywhere()] * 2 + [vmem()] * 2,
        scratch_shapes=[
            sea_scratch,
            scratch(amount_sea, 1, cells, dtype=I32),
            sea_scratch,
            sea_marks_in,
            scratch(levels_sea, cells, dtype=BF16),
            counts_in,
            counts_in,
            dma((3,)),
            dma((2,)),
        ],
        compiler_params=params,
        cost_estimate=pl.CostEstimate(flops=8 * 10**9, bytes_accessed=10**7, transcendentals=0),
        name="sea_own",
    )(payload, sea, in_hbm(ocn_nbrs.reshape(amount_sea, 1, cells)), counts, weights)
    sea_next, mapped = pl.pallas_call(
        functools.partial(last_kernel, atm_groups, amount_sea),
        out_shape=[sea_shape, shape((ret_fields, 1, columns), F32)],
        in_specs=[vmem()] * 3 + [anywhere()] * 5 + [vmem()] * 2 + [anywhere()] * 3,
        out_specs=[anywhere()] * 2,
        scratch_shapes=[
            scratch(fields, row_count),
            scratch(ret_fields, 1, columns),
            owner_in,
            pltpu.SMEM((groups - atm_groups,), I32),
            recv_in,
            sea_scratch,
            sea_scratch,
            sea_marks_in,
            scratch(1, cells),
            scratch(fields, levels_sea),
            dma((6,)),
            dma((2,)),
        ],
        input_output_aliases={12: 0},
        compiler_params=params,
        name="last",
    )(
        arrived, back_tiles, weights_back, owner,
        recv, sea, in_hbm(sums), sea_marks, sea_first, sea_second, in_hbm(ocn_mix.reshape(1, cells)), in_hbm(force_weight.T),
        sea_pre,
    )
    mapped = mapped.reshape(1, 1, ret_fields, columns)
    return (air_next[None, None], sea_next[None, None], mapped)


def solution(mesh):
    whole = P("grp", "dev")
    specs = [whole] * 15
    for replicated in (4, 13, 14):
        specs[replicated] = P()
    return jax.shard_map(
        on_device,
        mesh=mesh,
        in_specs=tuple(specs),
        out_specs=(whole, whole, whole),
        check_vma=False,
    )
```

```python
import functools

import jax
import jax.numpy as jnp
from jax import lax
from jax.experimental import pallas as pl
from jax.experimental.pallas import tpu as pltpu
from jax.sharding import PartitionSpec as P

F32 = jnp.float32
BF16 = jnp.bfloat16
I32 = jnp.int32
I16 = jnp.int16
TILE = 256
NT = (((1,), (1,)), ((), ()))


def dot(a, b):
    return jnp.dot(a, b, preferred_element_type=F32)


def dot_nt(a, b):
    return lax.dot_general(a, b, NT, preferred_element_type=F32)


def split(x):
    hi = x.astype(BF16)
    lo = (x - hi.astype(F32)).astype(BF16)
    return hi, lo


def exact(w, x):
    wh, wl = split(w)
    xh, xl = split(x)
    return dot(wh, xh) + (dot(wl, xh) + dot(wh, xl))


def row_iota(rows, cols):
    return lax.broadcasted_iota(I32, (rows, cols), 0)


def one_hot(rows_bf, index_row):
    return jnp.where(rows_bf == index_row, jnp.ones((), BF16), jnp.zeros((), BF16))


def cast_row(row):
    return row.astype(F32).astype(BF16)


def row_marks(rows, cols):
    return cast_row(row_iota(rows, cols))


def marks_at(picks, base, rows):
    marks = None
    for pick in picks:
        mark = one_hot(rows, cast_row(pick - base))
        marks = mark if marks is None else marks + mark
    return marks


def is_even():
    return lax.rem(lax.axis_index("dev"), 2) == 0


def pack_into(state, send, first, second):
    half = first.shape[1]
    rows = row_marks(TILE, 2 * half)
    index = send[...]
    total = None
    for base in range(0, state.shape[1], TILE):
        part = dot(state[:, base : base + TILE].astype(BF16), marks_at([index], base, rows))
        total = part if total is None else total + part
    down = total[:, :half]
    up = total[:, half:]
    even = is_even()
    first[...] = jnp.where(even, down, up).astype(BF16)
    second[...] = jnp.where(even, up, down).astype(BF16)


def rims(first, second):
    even = is_even()
    one = first[...].astype(F32)
    two = second[...].astype(F32)
    both = jnp.concatenate([jnp.where(even, one, two), jnp.where(even, two, one)], axis=1)
    return both.astype(BF16)


def fetch(source, target, sem):
    copy = pltpu.make_async_copy(source, target, sem)
    copy.start()
    return copy


def fetch_all(pairs, sems):
    return [fetch(source, target, sems.at[i]) for i, (source, target) in enumerate(pairs)]


def wait_all(copies):
    for copy in copies:
        copy.wait()


def air_pack_kernel(atm_groups, air_ref, send_ref, down, up, air, send, sems):
    @pl.when(lax.axis_index("grp") < atm_groups)
    def _():
        wait_all(fetch_all([(send_ref, send), (air_ref, air)], sems))
        pack_into(air, send, down, up)


def sums_of(pool, nbrs, at, width):
    rows = row_marks(TILE, width)
    picks = [n[:, pl.ds(at, width)] for n in nbrs]
    total = None
    for base in range(0, pool.shape[1], TILE):
        part = dot(pool[:, base : base + TILE], marks_at(picks, base, rows))
        total = part if total is None else total + part
    return total


def rim_marks(nbrs, at, width, own):
    picks = [n[:, pl.ds(at, width)] for n in nbrs]
    return marks_at(picks, own, row_marks(TILE, width))


def fill_ends(counts, ends):
    blocks, lanes = counts.shape
    given = cast_row(counts[...])
    upto = jnp.where(
        row_iota(lanes, lanes) <= lax.broadcasted_iota(I32, (lanes, lanes), 1), 1.0, 0.0
    ).astype(BF16)
    within = dot(given, upto)
    whole = dot(given, jnp.ones((lanes, lanes), BF16))
    before = jnp.zeros((1, lanes), F32)
    for j in range(blocks):
        ends[j : j + 1, :] = (within[j : j + 1] + before).astype(I32)
        before = before + whole[j : j + 1]


def interval(order, begin, end):
    return jnp.where((order >= begin) & (order < end), jnp.ones((), BF16), jnp.zeros((), BF16))


def fill_limits(counts, ends, begins_at, ends_at):
    blocks, lanes = counts.shape
    end = jnp.transpose(ends[...].astype(F32)).astype(I32)
    begin = jnp.transpose((ends[...] - counts[...]).astype(F32)).astype(I32)
    for j in range(blocks):
        at = slice(j * lanes, (j + 1) * lanes)
        ends_at[at, :] = jnp.broadcast_to(end[:, j : j + 1], (lanes, lanes)).astype(I16)
        begins_at[at, :] = jnp.broadcast_to(begin[:, j : j + 1], (lanes, lanes)).astype(I16)


def spans(columns):
    reach = (columns // 2) // TILE
    amount = columns // TILE
    return [
        (p, list(range(max(0, p - reach), min(p, amount - 1) + 1))) for p in range(amount + reach)
    ]


def fill_spread(begins_at, ends_at, tiles):
    columns, lanes = ends_at.shape
    lane = lax.broadcasted_iota(I32, (TILE, lanes), 1)
    i = 0
    for p, near in spans(columns):
        for t in near:
            at = slice(t * TILE, (t + 1) * TILE)
            for side in range(0, TILE, lanes):
                order = (lane + (p * TILE + side)).astype(I16)
                tiles[i * TILE : (i + 1) * TILE, side : side + lanes] = interval(
                    order, begins_at[at, :], ends_at[at, :]
                )
            i += 1


def fill_gather(counts, ends, tiles):
    blocks, lanes = counts.shape
    each = TILE // lanes
    limits = []
    for t in range(blocks // each):
        lines = range(t * each, (t + 1) * each)
        end = jnp.concatenate([ends[i : i + 1, :] for i in lines], axis=1)
        count = jnp.concatenate([counts[i : i + 1, :] for i in lines], axis=1)
        limits.append(((end - count).astype(I16), end.astype(I16)))
    rows = row_iota(TILE, TILE)
    i = 0
    for p, near in spans(blocks * lanes):
        order = (rows + p * TILE).astype(I16)
        for t in near:
            tiles[i * TILE : (i + 1) * TILE, :] = interval(order, *limits[t])
            i += 1


def slots_of(owner, seen, visit):
    for o in range(seen.shape[0]):
        seen[o] = 0
    for b in range(owner.shape[1]):
        o = owner[0, b]
        k = seen[o]
        seen[o] = k + 1
        visit(b, o, k)


def look_up(sea, ret_weight, recv, returned, looked):
    cells = sea.shape[1]
    fields = ret_weight.shape[0]
    his = cells // TILE
    pad = returned.shape[0] // his
    for h in range(his):
        chunk = exact(ret_weight[...], sea[:, h * TILE : (h + 1) * TILE])
        chunk = jnp.concatenate([chunk, jnp.zeros((pad - fields, TILE), F32)], axis=0)
        returned[h * pad : (h + 1) * pad, :] = chunk.astype(BF16)
    senders, slots, block = recv.shape
    for s in range(senders):
        index = jnp.concatenate([recv[s, k : k + 1, :] for k in range(slots)], axis=1)
        top = index // TILE
        rest = cast_row(index - top * TILE)
        found = dot(returned[...], one_hot(row_marks(TILE, slots * block), rest))
        look = jnp.zeros((pad, slots * block), F32)
        for h in range(his):
            look = jnp.where(top == h, found[h * pad : (h + 1) * pad], look)
        look = jnp.concatenate(
            [look, jnp.zeros((looked.shape[2] - pad, slots * block), F32)], axis=0
        ).astype(BF16)
        for k in range(slots):
            looked[s, k] = look[:, k * block : (k + 1) * block]


def air_own_kernel(
    atm_groups,
    after, air_ref, air_nbrs_ref, air_mix_ref, counts_ref, flux_weight_ref, weights_ref,
    part_ref, marks_ref, rows_own, rim_rows, air_mix, flux_weight, weights,
    part, marks, air, air_nbrs, counts, ends, begins_at, ends_at, tiles, pool, values, scaled, sems, out_sems,
):
    @pl.when(lax.axis_index("grp") < atm_groups)
    def _():
        many, near, whole, mixed, *rest = fetch_all(
            [
                (counts_ref, counts),
                (air_nbrs_ref, air_nbrs),
                (air_ref, air),
                (air_mix_ref, air_mix),
                (flux_weight_ref, flux_weight),
                (weights_ref, weights),
            ],
            sems,
        )
        amount, columns = air_nbrs.shape
        nbrs = [air_nbrs.at[k : k + 1, :] for k in range(amount)]
        many.wait()
        fill_ends(counts, ends)
        fill_limits(counts, ends, begins_at, ends_at)
        fill_spread(begins_at, ends_at, tiles)
        near.wait()
        for at in range(0, columns, TILE):
            marks[:, at : at + TILE] = rim_marks(nbrs, at, TILE, columns)
        wait_all([whole, mixed])
        pool[...] = air[...].astype(BF16)
        for at in range(0, columns, TILE):
            total = sums_of(pool, nbrs, at, TILE)
            own = air[:, at : at + TILE]
            mix = air_mix[:, at : at + TILE]
            part[:, at : at + TILE] = own + mix * (total * (1.0 / amount) - own)
            scaled[:, at : at + TILE] = (
                marks[:, at : at + TILE].astype(F32) * (mix * (1.0 / amount))
            ).astype(BF16)
        kept = fetch_all([(part, part_ref), (marks, marks_ref)], out_sems)
        wait_all(rest)
        fields = flux_weight.shape[0]
        values[...] = jnp.zeros(values.shape, BF16)
        for at in range(0, columns, TILE):
            hi, lo = split(exact(flux_weight[...], part[:, at : at + TILE]))
            values[0:fields, at : at + TILE] = hi
            values[32 : 32 + fields, at : at + TILE] = lo
        i = 0
        for p, near_by in spans(columns):
            both = None
            rim = None
            for t in near_by:
                at = slice(t * TILE, (t + 1) * TILE)
                mark = tiles[i * TILE : (i + 1) * TILE, :]
                more = dot(values[:, at], mark)
                more_rim = dot(scaled[:, at], mark)
                both = more if both is None else both + more
                rim = more_rim if rim is None else rim + more_rim
                i += 1
            at = slice(p * TILE, (p + 1) * TILE)
            rows_own[:, at] = both[0:fields] + both[32 : 32 + fields]
            rim_rows[:, at] = rim.astype(BF16)
        wait_all(kept)


def mid_kernel(
    atm_groups,
    first, second, rows_own, rim_rows, flux_weight, weights, air_ref, owner_ref,
    sea_ref, sea_send_ref, ret_weight_ref, recv_ref,
    payload, air_out, sea_down_ref, sea_up_ref,
    air, values, sent, owner, seen,
    sea, sea_send, ret_weight, recv, returned, down, up, sems, out_sems,
):
    here = lax.axis_index("grp") < atm_groups
    count_groups = sent.shape[0]

    @pl.when(here)
    def _():
        owned = fetch(owner_ref, owner, sems.at[0])
        sent[...] = jnp.zeros(sent.shape, BF16)
        values[...] = jnp.zeros(values.shape, BF16)
        rim = rims(first, second)
        fields = flux_weight.shape[0]
        high, rest = split(flux_weight[...])
        hi, lo = split(dot(high, rim) + dot(rest, rim))
        values[0:fields, :] = hi
        values[32 : 32 + fields, :] = lo
        block = sent.shape[3]
        each = TILE // block
        made = []
        for p in range(weights.shape[1] // TILE):
            at = slice(p * TILE, (p + 1) * TILE)
            both = dot(values[...], rim_rows[:, at])
            tile = (rows_own[:, at] + (both[0:fields] + both[32 : 32 + fields])) * weights[:, at]
            made.append(tile.astype(BF16))

        def visit(b, o, k):
            i = b % each
            sent[o, k] = made[b // each][:, i * block : (i + 1) * block]

        owned.wait()
        slots_of(owner, seen, visit)
        done = fetch(sent, payload.at[pl.ds(atm_groups, count_groups)], out_sems.at[1])
        done.wait()

    @pl.when(jnp.logical_not(here))
    def _():
        listed, kept, *rest = fetch_all(
            [
                (sea_send_ref, sea_send),
                (air_ref, air),
                (sea_ref, sea),
                (ret_weight_ref, ret_weight),
                (recv_ref, recv),
            ],
            sems,
        )
        wait_all(rest)
        look_up(sea, ret_weight, recv, returned, sent)
        done = fetch(sent, payload.at[pl.ds(0, atm_groups)], out_sems.at[1])
        kept.wait()
        keep = fetch(air, air_out, out_sems.at[0])
        listed.wait()
        pack_into(sea, sea_send, down, up)
        out_down = fetch(down, sea_down_ref, out_sems.at[2])
        out_up = fetch(up, sea_up_ref, out_sems.at[3])
        wait_all([done, keep, out_down, out_up])


def sea_own_kernel(
    atm_groups, amount_air,
    after, sea_ref, sea_nbrs_ref, counts_ref, weights_ref, first, second, part_ref, air_marks_ref, air_mix, air_in, sea_first_in, sea_second_in,
    sums_ref, marks_ref, sea_out, tiles, weights, air_out, sea_first, sea_second,
    sea, sea_nbrs, sums, marks, pool, counts, ends, air, part, air_marks, sems, out_sems,
):
    here = lax.axis_index("grp") < atm_groups

    @pl.when(here)
    def _():
        near, parted, whole, many, given = fetch_all(
            [
                (air_marks_ref, air_marks),
                (part_ref, part),
                (sea_ref, sea),
                (counts_ref, counts),
                (weights_ref, weights),
            ],
            sems,
        )
        wait_all([near, parted])
        rim = rims(first, second)
        for at in range(0, air.shape[1], TILE):
            total = dot(rim, air_marks[:, at : at + TILE])
            air[:, at : at + TILE] = part[:, at : at + TILE] + air_mix[:, at : at + TILE] * (
                total * (1.0 / amount_air)
            )
        stored = fetch(air, air_out, out_sems.at[1])
        whole.wait()
        keep = fetch(sea, sea_out, out_sems.at[0])
        many.wait()
        fill_ends(counts, ends)
        fill_gather(counts, ends, tiles)
        wait_all([given, keep, stored])

    @pl.when(jnp.logical_not(here))
    def _():
        near, whole = fetch_all([(sea_nbrs_ref, sea_nbrs), (sea_ref, sea)], sems)
        amount, _, cells = sea_nbrs.shape
        nbrs = [sea_nbrs.at[k] for k in range(amount)]
        near.wait()
        for at in range(0, cells, TILE):
            marks[:, at : at + TILE] = rim_marks(nbrs, at, TILE, cells)
        out_marks = fetch(marks, marks_ref, out_sems.at[1])
        whole.wait()
        pool[...] = sea[...].astype(BF16)

        def step(i, carry):
            at = pl.multiple_of(i * TILE, TILE)
            sums[:, pl.ds(at, TILE)] = sums_of(pool, nbrs, at, TILE)
            return carry

        lax.fori_loop(0, cells // TILE, step, 0)
        out_sums = fetch(sums, sums_ref, out_sems.at[0])
        wait_all([out_marks, out_sums])


def last_kernel(
    atm_groups, amount,
    arrived, tiles, weights, owner_ref,
    recv_ref, sea_ref, sums_ref, marks_ref, first, second, sea_mix_ref, force_weight_ref, sea_in,
    sea_out, mapped_ref,
    mine, mapped, owner, seen,
    recv, sea, sums, marks, sea_mix, force_weight, sems, out_sems,
):
    here = lax.axis_index("grp") < atm_groups
    fields, _, columns = mapped.shape

    @pl.when(here)
    def _():
        owned = fetch(owner_ref, owner, sems.at[0])
        block = arrived.shape[3]

        def visit(b, o, k):
            mine[:, b * block : (b + 1) * block] = arrived[atm_groups + o, k].astype(F32)

        owned.wait()
        slots_of(owner, seen, visit)
        w = weights[...]
        scaled = mine[0:16, :] * w
        order = row_iota(16, scaled.shape[1])
        scaled = jnp.where(order < fields, scaled, jnp.where(order == fields, w, 0.0))
        hi, lo = split(scaled)
        both_in = jnp.concatenate([hi, lo], axis=0)
        sums_in = [None] * (columns // TILE)
        i = 0
        for p, near in spans(columns):
            for t in near:
                more = dot(both_in[:, p * TILE : (p + 1) * TILE], tiles[i * TILE : (i + 1) * TILE, :])
                sums_in[t] = more if sums_in[t] is None else sums_in[t] + more
                i += 1
        for t, both in enumerate(sums_in):
            both = both[0:16] + both[16:32]
            mean = both[0:fields] / both[fields : fields + 1]
            for f in range(fields):
                mapped[f, :, t * TILE : (t + 1) * TILE] = mean[f : f + 1]
        fetch(mapped, mapped_ref, out_sems.at[0]).wait()

    @pl.when(jnp.logical_not(here))
    def _():
        mapped[...] = jnp.zeros(mapped.shape, F32)
        stored = fetch(mapped, mapped_ref, out_sems.at[0])
        cells_in, *rest = fetch_all(
            [
                (recv_ref, recv),
                (sea_ref, sea),
                (sums_ref, sums),
                (marks_ref, marks),
                (sea_mix_ref, sea_mix),
                (force_weight_ref, force_weight),
            ],
            sems,
        )
        senders, slots, block = recv.shape
        rows = arrived.shape[2]
        his = sea.shape[1] // TILE
        flux = jnp.zeros((his * rows, TILE), F32)
        cells_in.wait()
        for s in range(senders):
            index = jnp.concatenate([recv[s, k : k + 1, :] for k in range(slots)], axis=1)
            top = index // TILE
            rest_of = cast_row(index - top * TILE)
            values = jnp.concatenate([arrived[s, k].astype(F32) for k in range(slots)], axis=1)
            parts = [jnp.where(top == h, values, 0.0) for h in range(his)]
            apart = jnp.concatenate(parts, axis=0).astype(BF16)
            flux = flux + dot_nt(apart, one_hot(row_marks(TILE, slots * block), rest_of))
        wait_all(rest)
        rim = rims(first, second)
        spread_weight = jnp.transpose(force_weight[...])
        for h in range(his):
            at = slice(h * TILE, (h + 1) * TILE)
            forcing = exact(spread_weight, flux[h * rows : (h + 1) * rows])
            total = sums[:, at] + dot(rim, marks[:, at])
            own = sea[:, at]
            sea[:, at] = own + sea_mix[:, at] * (total * (1.0 / amount) - own) + forcing
        out = fetch(sea, sea_out, out_sems.at[1])
        wait_all([stored, out])


def vmem():
    return pl.BlockSpec(memory_space=pltpu.VMEM)


def anywhere():
    return pl.BlockSpec(memory_space=pl.ANY)


def in_hbm(x):
    return pltpu.with_memory_space_constraint(x, pltpu.HBM)


def shape(dims, dtype):
    return jax.ShapeDtypeStruct(dims, dtype)


def on_device(
    atm_state, atm_nbrs, atm_send, atm_mix, flux_weight, margin_counts, margin_weight,
    block_owner, recv_cols, ocn_state, ocn_nbrs, ocn_send, ocn_mix, force_weight, ret_weight,
):
    levels_air, columns = atm_state.shape[2:]
    levels_sea, cells = ocn_state.shape[2:]
    pair = atm_send.shape[2]
    half = pair // 2
    amount_air = atm_nbrs.shape[2]
    amount_sea = ocn_nbrs.shape[2]
    atm_groups, capacity, block = recv_cols.shape[2:]
    row_count = margin_weight.shape[2]
    blocks_here = block_owner.shape[2]
    fields = flux_weight.shape[0]
    ret_fields = ret_weight.shape[0]
    groups = lax.axis_size("grp")
    peers = lax.axis_size("dev")

    air = in_hbm(atm_state.reshape(levels_air, columns))
    sea = in_hbm(ocn_state.reshape(levels_sea, cells))
    counts = in_hbm(margin_counts.reshape(columns // 128, 128))
    weights = in_hbm(margin_weight.reshape(1, row_count))
    owner = in_hbm(block_owner.reshape(1, blocks_here))
    recv = in_hbm(recv_cols.reshape(atm_groups, capacity, block))
    air_mix = in_hbm(atm_mix.reshape(1, columns))
    air_shape = shape((levels_air, columns), F32)
    sea_shape = shape((levels_sea, cells), F32)
    air_rim = shape((levels_air, half), BF16)
    sea_rim = shape((levels_sea, half), BF16)
    payload_shape = shape((groups, capacity, fields, block), BF16)
    sent_shape = (capacity, fields, block)
    dma = pltpu.SemaphoreType.DMA
    tile_count = sum(len(near) for _, near in spans(columns))
    tiles_shape = shape((tile_count * TILE, TILE), BF16)
    owner_in = pltpu.SMEM((1, blocks_here), I32)

    def scratch(*dims, dtype=F32):
        return pltpu.VMEM(dims, dtype)

    air_scratch = scratch(levels_air, columns)
    sea_scratch = scratch(levels_sea, cells)
    sea_marks_in = scratch(pair, cells, dtype=BF16)
    counts_in = scratch(columns // 128, 128, dtype=I32)
    sea_half = scratch(levels_sea, half, dtype=BF16)
    pair_in = scratch(1, pair, dtype=I32)
    recv_in = scratch(atm_groups, capacity, block, dtype=I32)
    params = pltpu.CompilerParams(vmem_limit_bytes=24 * 2**20)
    wide = pltpu.CompilerParams(vmem_limit_bytes=24 * 2**20)

    def swapped(value, first, last, odd):
        pairs = [
            (g * peers + i, g * peers + (((i - odd) ^ 1) + odd) % peers)
            for g in range(first, last)
            for i in range(peers)
        ]
        return lax.ppermute(value, ("grp", "dev"), pairs)

    to_first, to_second = pl.pallas_call(
        functools.partial(air_pack_kernel, atm_groups),
        out_shape=[air_rim] * 2,
        in_specs=[anywhere()] * 2,
        out_specs=[vmem(), vmem()],
        scratch_shapes=[air_scratch, pair_in, dma((2,))],
        compiler_params=params,
        name="air_pack",
    )(air, in_hbm(atm_send.reshape(1, pair)))
    first = swapped(to_first, 0, atm_groups, 1)
    second = swapped(to_second, 0, atm_groups, 0)

    part, marks, rows_own, rim_rows, mix, flux_in, weights_here = pl.pallas_call(
        functools.partial(air_own_kernel, atm_groups),
        out_shape=[
            air_shape,
            shape((pair, columns), BF16),
            shape((fields, row_count), F32),
            shape((pair, row_count), BF16),
            shape((1, columns), F32),
            shape((fields, levels_air), F32),
            shape((1, row_count), F32),
        ],
        in_specs=[anywhere()] * 7,
        out_specs=[anywhere()] * 2 + [vmem()] * 5,
        scratch_shapes=[
            air_scratch,
            scratch(pair, columns, dtype=BF16),
            air_scratch,
            scratch(amount_air, columns, dtype=I32),
            counts_in,
            counts_in,
            scratch(columns, 128, dtype=I16),
            scratch(columns, 128, dtype=I16),
            scratch(tile_count * TILE, TILE, dtype=BF16),
            scratch(levels_air, columns, dtype=BF16),
            scratch(64, columns, dtype=BF16),
            scratch(pair, columns, dtype=BF16),
            dma((6,)),
            dma((2,)),
        ],
        compiler_params=wide,
        cost_estimate=pl.CostEstimate(flops=4 * 10**9, bytes_accessed=10**7, transcendentals=0),
        name="air_own",
    )(
        to_first, air, in_hbm(atm_nbrs.reshape(amount_air, columns)), air_mix, counts,
        in_hbm(flux_weight), weights,
    )
    payload, air_pre, sea_to_first, sea_to_second = pl.pallas_call(
        functools.partial(mid_kernel, atm_groups),
        out_shape=[payload_shape, air_shape, sea_rim, sea_rim],
        in_specs=[vmem()] * 6 + [anywhere()] * 6,
        out_specs=[anywhere()] * 4,
        scratch_shapes=[
            air_scratch,
            scratch(64, pair, dtype=BF16),
            scratch(atm_groups, *sent_shape, dtype=BF16),
            owner_in,
            pltpu.SMEM((groups - atm_groups,), I32),
            sea_scratch,
            pair_in,
            scratch(ret_fields, levels_sea),
            recv_in,
            scratch(16 * (cells // TILE), TILE, dtype=BF16),
            sea_half,
            sea_half,
            dma((5,)),
            dma((4,)),
        ],
        compiler_params=params,
        name="mid",
    )(
        first, second, rows_own, rim_rows, flux_in, weights_here, air, owner, sea, in_hbm(ocn_send.reshape(1, pair)), in_hbm(ret_weight), recv,
    )
    arrived = lax.all_to_all(payload, "grp", split_axis=0, concat_axis=0, tiled=True)

    sums, sea_marks, sea_pre, back_tiles, weights_back, air_next, *sea_sent = pl.pallas_call(
        functools.partial(sea_own_kernel, atm_groups, amount_air),
        out_shape=[
            sea_shape,
            shape((pair, cells), BF16),
            sea_shape,
            tiles_shape,
            shape((1, row_count), F32),
            air_shape,
            sea_rim,
            sea_rim,
        ],
        in_specs=[anywhere()] * 5 + [vmem()] * 2 + [anywhere()] * 2 + [vmem()] + [anywhere()] * 3,
        out_specs=[pl.BlockSpec(memory_space=pltpu.HBM)]
        + [anywhere()] * 2
        + [vmem()] * 2
        + [anywhere()] * 3,
        input_output_aliases={10: 5, 11: 6, 12: 7},
        scratch_shapes=[
            sea_scratch,
            scratch(amount_sea, 1, cells, dtype=I32),
            sea_scratch,
            sea_marks_in,
            scratch(levels_sea, cells, dtype=BF16),
            counts_in,
            counts_in,
            air_scratch,
            air_scratch,
            scratch(pair, columns, dtype=BF16),
            dma((5,)),
            dma((2,)),
        ],
        compiler_params=params,
        cost_estimate=pl.CostEstimate(flops=8 * 10**9, bytes_accessed=10**7, transcendentals=0),
        name="sea_own",
    )(
        payload, sea, in_hbm(ocn_nbrs.reshape(amount_sea, 1, cells)), counts, weights,
        first, second, in_hbm(part), in_hbm(marks), mix, air_pre,
        sea_to_first, sea_to_second,
    )
    sea_first = swapped(sea_sent[0], atm_groups, groups, 1)
    sea_second = swapped(sea_sent[1], atm_groups, groups, 0)
    sea_next, mapped = pl.pallas_call(
        functools.partial(last_kernel, atm_groups, amount_sea),
        out_shape=[sea_shape, shape((ret_fields, 1, columns), F32)],
        in_specs=[vmem()] * 3 + [anywhere()] * 5 + [vmem()] * 2 + [anywhere()] * 3,
        out_specs=[anywhere()] * 2,
        scratch_shapes=[
            scratch(fields, row_count),
            scratch(ret_fields, 1, columns),
            owner_in,
            pltpu.SMEM((groups - atm_groups,), I32),
            recv_in,
            sea_scratch,
            sea_scratch,
            sea_marks_in,
            scratch(1, cells),
            scratch(fields, levels_sea),
            dma((6,)),
            dma((2,)),
        ],
        input_output_aliases={12: 0},
        compiler_params=params,
        name="last",
    )(
        arrived, back_tiles, weights_back, owner,
        recv, sea, in_hbm(sums), sea_marks, sea_first, sea_second, in_hbm(ocn_mix.reshape(1, cells)), in_hbm(force_weight.T),
        sea_pre,
    )
    mapped = mapped.reshape(1, 1, ret_fields, columns)
    return (air_next[None, None], sea_next[None, None], mapped)


def solution(mesh):
    whole = P("grp", "dev")
    specs = [whole] * 15
    for replicated in (4, 13, 14):
        specs[replicated] = P()
    return jax.shard_map(
        on_device,
        mesh=mesh,
        in_specs=tuple(specs),
        out_specs=(whole, whole, whole),
        check_vma=False,
    )
```

```python
import functools

import jax
import jax.numpy as jnp
from jax import lax
from jax.experimental import pallas as pl
from jax.experimental.pallas import tpu as pltpu
from jax.sharding import PartitionSpec as P

F32 = jnp.float32
BF16 = jnp.bfloat16
I32 = jnp.int32
I16 = jnp.int16
TILE = 256
NT = (((1,), (1,)), ((), ()))


def dot(a, b):
    return jnp.dot(a, b, preferred_element_type=F32)


def dot_nt(a, b):
    return lax.dot_general(a, b, NT, preferred_element_type=F32)


def split(x):
    hi = x.astype(BF16)
    lo = (x - hi.astype(F32)).astype(BF16)
    return hi, lo


def exact(w, x):
    wh, wl = split(w)
    xh, xl = split(x)
    return dot(wh, xh) + (dot(wl, xh) + dot(wh, xl))


def row_iota(rows, cols):
    return lax.broadcasted_iota(I32, (rows, cols), 0)


def one_hot(rows_bf, index_row):
    return jnp.where(rows_bf == index_row, jnp.ones((), BF16), jnp.zeros((), BF16))


def cast_row(row):
    return row.astype(F32).astype(BF16)


def row_marks(rows, cols):
    return cast_row(row_iota(rows, cols))


def marks_at(picks, base, rows):
    marks = None
    for pick in picks:
        mark = one_hot(rows, cast_row(pick - base))
        marks = mark if marks is None else marks + mark
    return marks


def is_even():
    return lax.rem(lax.axis_index("dev"), 2) == 0


def pack_into(state, send, first, second, parts=()):
    half = first.shape[1]
    rows = row_marks(TILE, 2 * half)
    index = send[...]
    total = None
    for base in range(0, state.shape[1], TILE):
        marks = marks_at([index], base, rows)
        if parts:
            parts[base // TILE].wait()
        part = dot(state[:, base : base + TILE].astype(BF16), marks)
        total = part if total is None else total + part
    down = total[:, :half]
    up = total[:, half:]
    even = is_even()
    first[...] = jnp.where(even, down, up).astype(BF16)
    second[...] = jnp.where(even, up, down).astype(BF16)


def rims(first, second):
    even = is_even()
    one = first[...].astype(F32)
    two = second[...].astype(F32)
    both = jnp.concatenate([jnp.where(even, one, two), jnp.where(even, two, one)], axis=1)
    return both.astype(BF16)


def fetch(source, target, sem):
    copy = pltpu.make_async_copy(source, target, sem)
    copy.start()
    return copy


def fetch_all(pairs, sems):
    return [fetch(source, target, sems.at[i]) for i, (source, target) in enumerate(pairs)]


def wait_all(copies):
    for copy in copies:
        copy.wait()


def air_pack_kernel(atm_groups, air_ref, send_ref, down, up, air, send, sems):
    @pl.when(lax.axis_index("grp") < atm_groups)
    def _():
        pieces = [slice(at, at + TILE) for at in range(0, air.shape[1], TILE)]
        listed, *parts = fetch_all(
            [(send_ref, send)] + [(air_ref.at[:, at], air.at[:, at]) for at in pieces], sems
        )
        listed.wait()
        pack_into(air, send, down, up, parts)


def sums_of(pool, nbrs, at, width):
    rows = row_marks(TILE, width)
    picks = [n[:, pl.ds(at, width)] for n in nbrs]
    total = None
    for base in range(0, pool.shape[1], TILE):
        part = dot(pool[:, base : base + TILE], marks_at(picks, base, rows))
        total = part if total is None else total + part
    return total


def rim_marks(nbrs, at, width, own):
    picks = [n[:, pl.ds(at, width)] for n in nbrs]
    return marks_at(picks, own, row_marks(TILE, width))


def fill_ends(counts, ends):
    blocks, lanes = counts.shape
    given = cast_row(counts[...])
    upto = jnp.where(
        row_iota(lanes, lanes) <= lax.broadcasted_iota(I32, (lanes, lanes), 1), 1.0, 0.0
    ).astype(BF16)
    within = dot(given, upto)
    whole = dot(given, jnp.ones((lanes, lanes), BF16))
    before = jnp.zeros((1, lanes), F32)
    for j in range(blocks):
        ends[j : j + 1, :] = (within[j : j + 1] + before).astype(I32)
        before = before + whole[j : j + 1]


def interval(order, begin, end):
    return jnp.where((order >= begin) & (order < end), jnp.ones((), BF16), jnp.zeros((), BF16))


def fill_limits(counts, ends, begins_at, ends_at):
    blocks, lanes = counts.shape
    end = jnp.transpose(ends[...].astype(F32)).astype(I32)
    begin = jnp.transpose((ends[...] - counts[...]).astype(F32)).astype(I32)
    for j in range(blocks):
        at = slice(j * lanes, (j + 1) * lanes)
        ends_at[at, :] = jnp.broadcast_to(end[:, j : j + 1], (lanes, lanes)).astype(I16)
        begins_at[at, :] = jnp.broadcast_to(begin[:, j : j + 1], (lanes, lanes)).astype(I16)


def spans(columns):
    reach = (columns // 2) // TILE
    amount = columns // TILE
    return [
        (p, list(range(max(0, p - reach), min(p, amount - 1) + 1))) for p in range(amount + reach)
    ]


def fill_spread(begins_at, ends_at, tiles):
    columns, lanes = ends_at.shape
    lane = lax.broadcasted_iota(I32, (TILE, lanes), 1)
    i = 0
    for p, near in spans(columns):
        for t in near:
            at = slice(t * TILE, (t + 1) * TILE)
            for side in range(0, TILE, lanes):
                order = (lane + (p * TILE + side)).astype(I16)
                tiles[i * TILE : (i + 1) * TILE, side : side + lanes] = interval(
                    order, begins_at[at, :], ends_at[at, :]
                )
            i += 1


def fill_gather(counts, ends, tiles):
    blocks, lanes = counts.shape
    each = TILE // lanes
    limits = []
    for t in range(blocks // each):
        lines = range(t * each, (t + 1) * each)
        end = jnp.concatenate([ends[i : i + 1, :] for i in lines], axis=1)
        count = jnp.concatenate([counts[i : i + 1, :] for i in lines], axis=1)
        limits.append(((end - count).astype(I16), end.astype(I16)))
    rows = row_iota(TILE, TILE)
    i = 0
    for p, near in spans(blocks * lanes):
        order = (rows + p * TILE).astype(I16)
        for t in near:
            tiles[i * TILE : (i + 1) * TILE, :] = interval(order, *limits[t])
            i += 1


def slots_of(owner, seen, visit):
    for o in range(seen.shape[0]):
        seen[o] = 0
    for b in range(owner.shape[1]):
        o = owner[0, b]
        k = seen[o]
        seen[o] = k + 1
        visit(b, o, k)


def look_up(sea, ret_weight, recv, returned, looked):
    cells = sea.shape[1]
    fields = ret_weight.shape[0]
    his = cells // TILE
    pad = returned.shape[0] // his
    for h in range(his):
        chunk = exact(ret_weight[...], sea[:, h * TILE : (h + 1) * TILE])
        chunk = jnp.concatenate([chunk, jnp.zeros((pad - fields, TILE), F32)], axis=0)
        returned[h * pad : (h + 1) * pad, :] = chunk.astype(BF16)
    senders, slots, block = recv.shape
    for s in range(senders):
        index = jnp.concatenate([recv[s, k : k + 1, :] for k in range(slots)], axis=1)
        top = index // TILE
        rest = cast_row(index - top * TILE)
        found = dot(returned[...], one_hot(row_marks(TILE, slots * block), rest))
        look = jnp.zeros((pad, slots * block), F32)
        for h in range(his):
            look = jnp.where(top == h, found[h * pad : (h + 1) * pad], look)
        look = jnp.concatenate(
            [look, jnp.zeros((looked.shape[2] - pad, slots * block), F32)], axis=0
        ).astype(BF16)
        for k in range(slots):
            looked[s, k] = look[:, k * block : (k + 1) * block]


def air_own_kernel(
    atm_groups,
    after, air_ref, air_nbrs_ref, air_mix_ref, counts_ref, flux_weight_ref, weights_ref,
    part, marks, tiles, air_mix, flux_weight, weights, payload,
    air, air_nbrs, counts, ends, begins_at, ends_at, pool, none, sems, out_sem,
):
    @pl.when(lax.axis_index("grp") < atm_groups)
    def _():
        many, near, whole, mixed, *rest = fetch_all(
            [
                (counts_ref, counts),
                (air_nbrs_ref, air_nbrs),
                (air_ref, air),
                (air_mix_ref, air_mix),
                (flux_weight_ref, flux_weight),
                (weights_ref, weights),
            ],
            sems,
        )
        none[...] = jnp.zeros(none.shape, BF16)
        cleared = fetch(none, payload.at[pl.ds(atm_groups, none.shape[0])], out_sem)
        amount, columns = air_nbrs.shape
        nbrs = [air_nbrs.at[k : k + 1, :] for k in range(amount)]
        many.wait()
        fill_ends(counts, ends)
        fill_limits(counts, ends, begins_at, ends_at)
        fill_spread(begins_at, ends_at, tiles)
        near.wait()
        for at in range(0, columns, TILE):
            marks[:, at : at + TILE] = rim_marks(nbrs, at, TILE, columns)
        wait_all([whole, mixed])
        pool[...] = air[...].astype(BF16)
        for at in range(0, columns, TILE):
            total = sums_of(pool, nbrs, at, TILE)
            own = air[:, at : at + TILE]
            mix = air_mix[:, at : at + TILE]
            part[:, at : at + TILE] = own + mix * (total * (1.0 / amount) - own)
        wait_all([*rest, cleared])


def mid_kernel(
    atm_groups, amount,
    first, second, part, marks, tiles, air_mix, flux_weight, weights, air_ref, owner_ref,
    sea_ref, sea_send_ref, ret_weight_ref, recv_ref, payload_in,
    payload, air_out, sea_down_ref, sea_up_ref,
    air, values, sent, blocks, owner, seen,
    sea, sea_send, ret_weight, recv, returned, down, up, sems, out_sems, block_sems,
):
    here = lax.axis_index("grp") < atm_groups

    @pl.when(here)
    def _():
        owned = fetch(owner_ref, owner, sems.at[0])
        values[...] = jnp.zeros(values.shape, BF16)
        rim = rims(first, second)
        columns = air.shape[1]
        fields = flux_weight.shape[0]
        for at in range(0, columns, TILE):
            total = dot(rim, marks[:, at : at + TILE])
            new = part[:, at : at + TILE] + air_mix[:, at : at + TILE] * (total * (1.0 / amount))
            air[:, at : at + TILE] = new
            hi, lo = split(exact(flux_weight[...], new))
            values[0:fields, at : at + TILE] = hi
            values[32 : 32 + fields, at : at + TILE] = lo
        stored = fetch(air, air_out, out_sems.at[0])
        block = sent.shape[3]
        each = TILE // block
        owned.wait()
        places = []
        slots_of(owner, seen, lambda b, o, k: places.append((o, k)))
        copies = [stored]
        i = 0
        for p, near in spans(columns):
            both = None
            for t in near:
                one = values[:, t * TILE : (t + 1) * TILE]
                more = dot(one, tiles[i * TILE : (i + 1) * TILE, :])
                both = more if both is None else both + more
                i += 1
            tile = (both[0:fields] + both[32 : 32 + fields]) * weights[:, p * TILE : (p + 1) * TILE]
            tile = tile.astype(BF16)
            for side in range(each):
                b = p * each + side
                o, k = places[b]
                blocks[b] = tile[:, side * block : (side + 1) * block]
                copies.append(fetch(blocks.at[b], payload.at[atm_groups + o, k], block_sems.at[b]))
        wait_all(copies)

    @pl.when(jnp.logical_not(here))
    def _():
        listed, kept, *rest = fetch_all(
            [
                (sea_send_ref, sea_send),
                (air_ref, air),
                (sea_ref, sea),
                (ret_weight_ref, ret_weight),
                (recv_ref, recv),
            ],
            sems,
        )
        wait_all(rest)
        look_up(sea, ret_weight, recv, returned, sent)
        done = fetch(sent, payload.at[pl.ds(0, atm_groups)], out_sems.at[1])
        kept.wait()
        keep = fetch(air, air_out, out_sems.at[0])
        listed.wait()
        pack_into(sea, sea_send, down, up)
        out_down = fetch(down, sea_down_ref, out_sems.at[2])
        out_up = fetch(up, sea_up_ref, out_sems.at[3])
        wait_all([done, keep, out_down, out_up])


def sea_own_kernel(
    atm_groups,
    after, sea_ref, sea_nbrs_ref, counts_ref, weights_ref,
    sums_ref, marks_ref, sea_out, tiles, weights,
    sea, sea_nbrs, sums, marks, pool, counts, ends, sems, out_sems,
):
    here = lax.axis_index("grp") < atm_groups

    @pl.when(here)
    def _():
        whole, many, given = fetch_all(
            [(sea_ref, sea), (counts_ref, counts), (weights_ref, weights)], sems
        )
        whole.wait()
        keep = fetch(sea, sea_out, out_sems.at[0])
        many.wait()
        fill_ends(counts, ends)
        fill_gather(counts, ends, tiles)
        wait_all([given, keep])

    @pl.when(jnp.logical_not(here))
    def _():
        near, whole = fetch_all([(sea_nbrs_ref, sea_nbrs), (sea_ref, sea)], sems)
        amount, _, cells = sea_nbrs.shape
        nbrs = [sea_nbrs.at[k] for k in range(amount)]
        near.wait()
        for at in range(0, cells, TILE):
            marks[:, at : at + TILE] = rim_marks(nbrs, at, TILE, cells)
        out_marks = fetch(marks, marks_ref, out_sems.at[1])
        whole.wait()
        pool[...] = sea[...].astype(BF16)

        def step(i, carry):
            at = pl.multiple_of(i * TILE, TILE)
            sums[:, pl.ds(at, TILE)] = sums_of(pool, nbrs, at, TILE)
            return carry

        lax.fori_loop(0, cells // TILE, step, 0)
        out_sums = fetch(sums, sums_ref, out_sems.at[0])
        wait_all([out_marks, out_sums])


def last_kernel(
    atm_groups, amount,
    arrived, tiles, weights, owner_ref,
    recv_ref, sea_ref, sums_ref, marks_ref, first, second, sea_mix_ref, force_weight_ref, sea_in,
    sea_out, mapped_ref,
    mine, mapped, owner, seen,
    recv, sea, sums, marks, sea_mix, force_weight, sems, out_sems,
):
    here = lax.axis_index("grp") < atm_groups
    fields, _, columns = mapped.shape

    @pl.when(here)
    def _():
        owned = fetch(owner_ref, owner, sems.at[0])
        block = arrived.shape[3]

        def visit(b, o, k):
            mine[:, b * block : (b + 1) * block] = arrived[atm_groups + o, k].astype(F32)

        owned.wait()
        slots_of(owner, seen, visit)
        w = weights[...]
        scaled = mine[0:16, :] * w
        order = row_iota(16, scaled.shape[1])
        scaled = jnp.where(order < fields, scaled, jnp.where(order == fields, w, 0.0))
        hi, lo = split(scaled)
        both_in = jnp.concatenate([hi, lo], axis=0)
        sums_in = [None] * (columns // TILE)
        i = 0
        for p, near in spans(columns):
            for t in near:
                more = dot(both_in[:, p * TILE : (p + 1) * TILE], tiles[i * TILE : (i + 1) * TILE, :])
                sums_in[t] = more if sums_in[t] is None else sums_in[t] + more
                i += 1
        for t, both in enumerate(sums_in):
            both = both[0:16] + both[16:32]
            mean = both[0:fields] / both[fields : fields + 1]
            for f in range(fields):
                mapped[f, :, t * TILE : (t + 1) * TILE] = mean[f : f + 1]
        fetch(mapped, mapped_ref, out_sems.at[0]).wait()

    @pl.when(jnp.logical_not(here))
    def _():
        mapped[...] = jnp.zeros(mapped.shape, F32)
        stored = fetch(mapped, mapped_ref, out_sems.at[0])
        cells_in, *rest = fetch_all(
            [
                (recv_ref, recv),
                (sea_ref, sea),
                (sums_ref, sums),
                (marks_ref, marks),
                (sea_mix_ref, sea_mix),
                (force_weight_ref, force_weight),
            ],
            sems,
        )
        senders, slots, block = recv.shape
        rows = arrived.shape[2]
        his = sea.shape[1] // TILE
        flux = jnp.zeros((his * rows, TILE), F32)
        cells_in.wait()
        for s in range(senders):
            index = jnp.concatenate([recv[s, k : k + 1, :] for k in range(slots)], axis=1)
            top = index // TILE
            rest_of = cast_row(index - top * TILE)
            values = jnp.concatenate([arrived[s, k].astype(F32) for k in range(slots)], axis=1)
            parts = [jnp.where(top == h, values, 0.0) for h in range(his)]
            apart = jnp.concatenate(parts, axis=0).astype(BF16)
            flux = flux + dot_nt(apart, one_hot(row_marks(TILE, slots * block), rest_of))
        wait_all(rest)
        rim = rims(first, second)
        spread_weight = jnp.transpose(force_weight[...])
        for h in range(his):
            at = slice(h * TILE, (h + 1) * TILE)
            forcing = exact(spread_weight, flux[h * rows : (h + 1) * rows])
            total = sums[:, at] + dot(rim, marks[:, at])
            own = sea[:, at]
            sea[:, at] = own + sea_mix[:, at] * (total * (1.0 / amount) - own) + forcing
        out = fetch(sea, sea_out, out_sems.at[1])
        wait_all([stored, out])


def vmem():
    return pl.BlockSpec(memory_space=pltpu.VMEM)


def anywhere():
    return pl.BlockSpec(memory_space=pl.ANY)


def in_hbm(x):
    return pltpu.with_memory_space_constraint(x, pltpu.HBM)


def shape(dims, dtype):
    return jax.ShapeDtypeStruct(dims, dtype)


def on_device(
    atm_state, atm_nbrs, atm_send, atm_mix, flux_weight, margin_counts, margin_weight,
    block_owner, recv_cols, ocn_state, ocn_nbrs, ocn_send, ocn_mix, force_weight, ret_weight,
):
    levels_air, columns = atm_state.shape[2:]
    levels_sea, cells = ocn_state.shape[2:]
    pair = atm_send.shape[2]
    half = pair // 2
    amount_air = atm_nbrs.shape[2]
    amount_sea = ocn_nbrs.shape[2]
    atm_groups, capacity, block = recv_cols.shape[2:]
    row_count = margin_weight.shape[2]
    blocks_here = block_owner.shape[2]
    fields = flux_weight.shape[0]
    ret_fields = ret_weight.shape[0]
    groups = lax.axis_size("grp")
    peers = lax.axis_size("dev")

    air = in_hbm(atm_state.reshape(levels_air, columns))
    sea = in_hbm(ocn_state.reshape(levels_sea, cells))
    counts = in_hbm(margin_counts.reshape(columns // 128, 128))
    weights = in_hbm(margin_weight.reshape(1, row_count))
    owner = in_hbm(block_owner.reshape(1, blocks_here))
    recv = in_hbm(recv_cols.reshape(atm_groups, capacity, block))
    air_mix = in_hbm(atm_mix.reshape(1, columns))
    air_shape = shape((levels_air, columns), F32)
    sea_shape = shape((levels_sea, cells), F32)
    air_rim = shape((levels_air, half), BF16)
    sea_rim = shape((levels_sea, half), BF16)
    payload_shape = shape((groups, capacity, fields, block), BF16)
    sent_shape = (capacity, fields, block)
    dma = pltpu.SemaphoreType.DMA
    tile_count = sum(len(near) for _, near in spans(columns))
    tiles_shape = shape((tile_count * TILE, TILE), BF16)
    owner_in = pltpu.SMEM((1, blocks_here), I32)

    def scratch(*dims, dtype=F32):
        return pltpu.VMEM(dims, dtype)

    air_scratch = scratch(levels_air, columns)
    sea_scratch = scratch(levels_sea, cells)
    sea_marks_in = scratch(pair, cells, dtype=BF16)
    counts_in = scratch(columns // 128, 128, dtype=I32)
    sea_half = scratch(levels_sea, half, dtype=BF16)
    pair_in = scratch(1, pair, dtype=I32)
    recv_in = scratch(atm_groups, capacity, block, dtype=I32)
    params = pltpu.CompilerParams(vmem_limit_bytes=24 * 2**20)

    def swapped(value, first, last, odd):
        pairs = [
            (g * peers + i, g * peers + (((i - odd) ^ 1) + odd) % peers)
            for g in range(first, last)
            for i in range(peers)
        ]
        return lax.ppermute(value, ("grp", "dev"), pairs)

    to_first, to_second = pl.pallas_call(
        functools.partial(air_pack_kernel, atm_groups),
        out_shape=[air_rim] * 2,
        in_specs=[anywhere()] * 2,
        out_specs=[vmem(), vmem()],
        scratch_shapes=[air_scratch, pair_in, dma((1 + columns // TILE,))],
        compiler_params=params,
        name="air_pack",
    )(air, in_hbm(atm_send.reshape(1, pair)))
    first = swapped(to_first, 0, atm_groups, 1)
    second = swapped(to_second, 0, atm_groups, 0)

    part, marks, tiles, mix, flux_in, weights_here, payload_in = pl.pallas_call(
        functools.partial(air_own_kernel, atm_groups),
        out_shape=[
            air_shape,
            shape((pair, columns), BF16),
            tiles_shape,
            shape((1, columns), F32),
            shape((fields, levels_air), F32),
            shape((1, row_count), F32),
            payload_shape,
        ],
        in_specs=[anywhere()] * 7,
        out_specs=[vmem()] * 6 + [anywhere()],
        scratch_shapes=[
            air_scratch,
            scratch(amount_air, columns, dtype=I32),
            counts_in,
            counts_in,
            scratch(columns, 128, dtype=I16),
            scratch(columns, 128, dtype=I16),
            scratch(levels_air, columns, dtype=BF16),
            scratch(groups - atm_groups, *sent_shape, dtype=BF16),
            dma((6,)),
            dma,
        ],
        compiler_params=params,
        cost_estimate=pl.CostEstimate(flops=4 * 10**9, bytes_accessed=10**7, transcendentals=0),
        name="air_own",
    )(
        to_second, air, in_hbm(atm_nbrs.reshape(amount_air, columns)), air_mix, counts,
        in_hbm(flux_weight), weights,
    )
    payload, air_next, sea_to_first, sea_to_second = pl.pallas_call(
        functools.partial(mid_kernel, atm_groups, amount_air),
        out_shape=[payload_shape, air_shape, sea_rim, sea_rim],
        in_specs=[vmem()] * 8 + [anywhere()] * 7,
        out_specs=[anywhere()] * 4,
        input_output_aliases={14: 0},
        scratch_shapes=[
            air_scratch,
            scratch(64, columns, dtype=BF16),
            scratch(atm_groups, *sent_shape, dtype=BF16),
            scratch(blocks_here, fields, block, dtype=BF16),
            owner_in,
            pltpu.SMEM((groups - atm_groups,), I32),
            sea_scratch,
            pair_in,
            scratch(ret_fields, levels_sea),
            recv_in,
            scratch(16 * (cells // TILE), TILE, dtype=BF16),
            sea_half,
            sea_half,
            dma((5,)),
            dma((4,)),
            dma((blocks_here,)),
        ],
        compiler_params=params,
        name="mid",
    )(
        first, second, part, marks, tiles, mix, flux_in, weights_here, air, owner, sea, in_hbm(ocn_send.reshape(1, pair)), in_hbm(ret_weight), recv, payload_in,
    )
    arrived = lax.all_to_all(payload, "grp", split_axis=0, concat_axis=0, tiled=True)
    sea_first = swapped(sea_to_first, atm_groups, groups, 1)
    sea_second = swapped(sea_to_second, atm_groups, groups, 0)

    sums, sea_marks, sea_pre, back_tiles, weights_back = pl.pallas_call(
        functools.partial(sea_own_kernel, atm_groups),
        out_shape=[
            sea_shape,
            shape((pair, cells), BF16),
            sea_shape,
            tiles_shape,
            shape((1, row_count), F32),
        ],
        in_specs=[anywhere()] * 5,
        out_specs=[pl.BlockSpec(memory_space=pltpu.HBM)] + [anywhere()] * 2 + [vmem()] * 2,
        scratch_shapes=[
            sea_scratch,
            scratch(amount_sea, 1, cells, dtype=I32),
            sea_scratch,
            sea_marks_in,
            scratch(levels_sea, cells, dtype=BF16),
            counts_in,
            counts_in,
            dma((3,)),
            dma((2,)),
        ],
        compiler_params=params,
        cost_estimate=pl.CostEstimate(flops=8 * 10**9, bytes_accessed=10**7, transcendentals=0),
        name="sea_own",
    )(payload, sea, in_hbm(ocn_nbrs.reshape(amount_sea, 1, cells)), counts, weights)
    sea_next, mapped = pl.pallas_call(
        functools.partial(last_kernel, atm_groups, amount_sea),
        out_shape=[sea_shape, shape((ret_fields, 1, columns), F32)],
        in_specs=[vmem()] * 3 + [anywhere()] * 5 + [vmem()] * 2 + [anywhere()] * 3,
        out_specs=[anywhere()] * 2,
        scratch_shapes=[
            scratch(fields, row_count),
            scratch(ret_fields, 1, columns),
            owner_in,
            pltpu.SMEM((groups - atm_groups,), I32),
            recv_in,
            sea_scratch,
            sea_scratch,
            sea_marks_in,
            scratch(1, cells),
            scratch(fields, levels_sea),
            dma((6,)),
            dma((2,)),
        ],
        input_output_aliases={12: 0},
        compiler_params=params,
        name="last",
    )(
        arrived, back_tiles, weights_back, owner,
        recv, sea, in_hbm(sums), sea_marks, sea_first, sea_second, in_hbm(ocn_mix.reshape(1, cells)), in_hbm(force_weight.T),
        sea_pre,
    )
    mapped = mapped.reshape(1, 1, ret_fields, columns)
    return (air_next[None, None], sea_next[None, None], mapped)


def solution(mesh):
    whole = P("grp", "dev")
    specs = [whole] * 15
    for replicated in (4, 13, 14):
        specs[replicated] = P()
    return jax.shard_map(
        on_device,
        mesh=mesh,
        in_specs=tuple(specs),
        out_specs=(whole, whole, whole),
        check_vma=False,
    )
```
